256 devices in a mesh: ctx: 32 (over y, x, core), head: 8 (over z).
Axes of the slice: x: 4, y: 4, z: 8, core: 2. Of those that a mesh axis runs over, the one named last changes fastest.
Arguments:
- queries: bfloat16 [32768, 4096], P('ctx', 'head'), may hold values from -1.796875 to 1.796875
- keys: bfloat16 [32768, 4096], P('ctx', 'head'), may hold values from -1.796875 to 1.796875
- values: bfloat16 [32768, 4096], P('ctx', 'head'), may hold values from -6 to 6
- gate: bfloat16 [32768, 4096], P('ctx', 'head'), may hold values from -6 to 6
- grad_out: bfloat16 [32768, 4096], P('ctx', 'head'), may hold values from -6 to 6
- gain: float32 [4096], P('head'), may hold values from 0.5 to 1.5
- decay_rate: float32 [32], P('head'), may hold values from 0 to 1, as said below
- segment_ids: int32 [32768], P('ctx'), may hold values from 0 to 15, never falling along the last dimension, each value on 1 to 8192 neighbouring positions
Outputs:
- grad_queries: bfloat16 [32768, 4096], P('ctx', 'head')
- grad_keys: bfloat16 [32768, 4096], P('ctx', 'head')
- grad_values: bfloat16 [32768, 4096], P('ctx', 'head')
- grad_gate: bfloat16 [32768, 4096], P('ctx', 'head')
- grad_gain: float32 [4096], P('head')
The draws below stay inside these ranges and needn't reach their ends.
Inputs may be any that keep to these rules, and one draw needn't show every extreme that they name: `segment_ids`: rollout ids never fall along the pack; each rollout holds at most 8192 tokens and one holds exactly 8192. `decay_rate`: positive rates.
All inputs are finite; a program needn't handle non-finite values.
Results may differ from the reference program's by a relative error of at most 0.0049.
Values sent between devices are 32-bit elements; how exact they have to be, the bound alone decides.
A program may use at most 128 MiB of HBM per device.

```python
import math
import jax
import jax.numpy as jnp
import numpy as np
from jax import lax

HEADS = 32
HD = 128
BLOCK = 256
ROLLOUTS = 16
TOKENS = 32768
MOST = 8192


def draw_decay_rate(key, part):
    key = jax.random.fold_in(key, 11)
    second = jax.random.fold_in(key, 1)
    slow_lo = jnp.log(0.5 / TOKENS)
    fast_hi = jnp.log(1.0 / 32.0)
    rates = jnp.exp(slow_lo + jax.random.uniform(second, (HEADS,)) * (fast_hi - slow_lo))
    return rates.astype(jnp.float32)


def steps_of(rng, extent, cuts, smallest, largest):
    def one(dim, shards_of):
        steps = jax.random.uniform(jax.random.fold_in(jax.random.fold_in(rng, 6), dim), (shards_of,), jnp.float32, smallest / len(cuts), largest / len(cuts))
        return jnp.repeat(jnp.exp(steps), extent[dim] // shards_of).reshape((-1,) + (1,) * (len(extent) - dim - 1))

    level = one(*cuts[0])
    for cut in cuts[1:]:
        level = level * one(*cut)
    return level


def split_up(amount, total, bound, slope):
    weights = [(1 << 20) // math.isqrt(grade ** slope) + 1 for grade in range(2, amount + 1)]
    spare, given = total - bound - (amount - 1), [1] * (amount - 1)
    while spare > 0:
        free = [i for i in range(amount - 1) if given[i] < bound]
        whole, budget = sum([weights[i] for i in free]), spare
        for i in free:
            addition = min(bound - given[i], max(1, budget * weights[i] // whole), spare)
            given[i] = given[i] + addition
            spare = spare - addition
    return np.array([bound] + given)


def ragged(rng, amount, total, reach, skew):
    if amount == 2:
        one = jax.random.randint(rng, (), max(1, total - reach), min(reach, total - 1) + 1)
        return jnp.stack([one, total - one])
    tallies = jnp.asarray(split_up(amount, total, reach, skew), jnp.int32)
    couples = (amount - 1) // 2
    source_of, taker = tallies[1:1 + 2 * couples:2], tallies[2:2 + 2 * couples:2]
    slack = jnp.minimum(source_of - 1, reach - taker)
    passed = jax.random.randint(jax.random.fold_in(rng, 1), (couples,), 0, 1 << 20) % (slack + 1)
    tallies = tallies.at[1:1 + 2 * couples:2].set(source_of - passed).at[2:2 + 2 * couples:2].set(taker + passed)
    return tallies[jax.random.permutation(jax.random.fold_in(rng, 2), amount)]


def centred(stream_key, shape, spread, limit, shards=(), held_as=jnp.bfloat16):
    entries = spread * jax.random.normal(stream_key, shape, jnp.float32)
    if shards:
        entries = entries * steps_of(stream_key, shape, shards, -0.22, 0.18)
    return jnp.clip(entries, -limit, limit).astype(held_as)


def setup_inputs(seed: int = 0) -> dict:
    streams_of = jax.random.split(jax.random.key(seed), 9)
    queries = centred(streams_of[0], (TOKENS, HEADS * HD), 0.3, 1.796875, ((0, 32), (1, 8)))
    keys = centred(streams_of[1], (TOKENS, HEADS * HD), 0.3, 1.796875, ((0, 32), (1, 8)))
    values = centred(streams_of[2], (TOKENS, HEADS * HD), 1.0, 6.0, ((0, 32), (1, 8)))
    gate = centred(streams_of[3], (TOKENS, HEADS * HD), 1.0, 6.0, ((0, 32), (1, 8)))
    grad_out = centred(streams_of[4], (TOKENS, HEADS * HD), 1.0, 6.0, ((0, 32), (1, 8)))
    gain = jnp.clip(1.0 + 0.1 * jax.random.normal(streams_of[5], (HEADS * HD,), jnp.float32), 0.5, 1.5)
    decay_rate = draw_decay_rate(jax.random.fold_in(streams_of[8], 71), 0)
    segment_ids = jnp.searchsorted(jnp.cumsum(ragged(streams_of[7], ROLLOUTS, TOKENS, MOST, 2)), jnp.arange(TOKENS), side="right").astype(jnp.int32)
    return dict(queries=queries, keys=keys, values=values, gate=gate, grad_out=grad_out, gain=gain, decay_rate=decay_rate, segment_ids=segment_ids)


def attend(qf, kf, vf, seg, rate):
    hi = lax.Precision.HIGHEST
    count = TOKENS // BLOCK
    qb = qf.reshape(count, BLOCK, HEADS, HD)
    kb = kf.reshape(count, BLOCK, HEADS, HD)
    vb = vf.reshape(count, BLOCK, HEADS, HD)
    sb = seg.reshape(count, BLOCK)
    logl = -rate
    pos = jnp.arange(BLOCK).astype(jnp.float32)
    diff = pos[:, None] - pos[None, :]
    causal = diff >= 0
    wbase = jnp.where(causal[None], jnp.exp(logl[:, None, None] * jnp.where(causal, diff, 0.0)[None]), 0.0)

    def step(carry, xs):
        state, label = carry
        qq, kk, vv, ss = xs
        same = (ss[:, None] == ss[None, :]).astype(jnp.float32)
        weights = wbase * same[None]
        scores = jnp.einsum('thd,shd->hts', qq, kk, precision=hi) * weights
        inner = jnp.einsum('hts,she->the', scores, vv, precision=hi)
        coef = jnp.exp(logl[None, :] * (pos + 1.0)[:, None]) * (ss == label).astype(jnp.float32)[:, None]
        cross = jnp.einsum('thd,hde->the', qq, state, precision=hi) * coef[:, :, None]
        final = ss[-1]
        keep = (final == label).astype(jnp.float32)
        wlast = jnp.exp(logl[None, :] * (BLOCK - 1.0 - pos)[:, None]) * (ss == final).astype(jnp.float32)[:, None]
        kw = kk * wlast[:, :, None]
        fresh = jnp.einsum('shd,she->hde', kw, vv, precision=hi)
        state = keep * jnp.exp(logl * BLOCK)[:, None, None] * state + fresh
        return ((state, final), inner + cross)
    init = (jnp.zeros((HEADS, HD, HD), jnp.float32), jnp.int32(-1))
    _, out = lax.scan(step, init, (qb, kb, vb, sb))
    return out.reshape(TOKENS, HEADS, HD)

def reference(queries, keys, values, gate, grad_out, gain, decay_rate, segment_ids):
    feats = HEADS * HD
    qf = queries.astype(jnp.float32).reshape(TOKENS, HEADS, HD)
    kf = keys.astype(jnp.float32).reshape(TOKENS, HEADS, HD)
    vf = values.astype(jnp.float32).reshape(TOKENS, HEADS, HD)

    def attn_fn(a, b, c):
        return attend(a, b, c, segment_ids, decay_rate)
    attn, pull = jax.vjp(attn_fn, qf, kf, vf)
    flat = attn.reshape(TOKENS, feats)
    ratio = lax.rsqrt(lax.optimization_barrier(jnp.mean(flat * flat, axis=-1, keepdims=True)) + 1e-06)
    normed = flat * ratio
    sig = jax.nn.sigmoid(gate.astype(jnp.float32))
    upper = grad_out.astype(jnp.float32)
    grad_gate = (upper * normed * gain * sig * (1.0 - sig)).astype(jnp.bfloat16)
    grad_gain = lax.optimization_barrier(jnp.sum(upper * sig * normed, axis=0))
    dz = upper * sig * gain
    cmean = lax.optimization_barrier(jnp.mean(dz * flat, axis=-1, keepdims=True))
    datt = (ratio * dz - ratio * ratio * ratio * cmean * flat).astype(jnp.bfloat16)
    dq, dk, dv = pull(datt.astype(jnp.float32).reshape(TOKENS, HEADS, HD))
    return (dq.reshape(TOKENS, feats).astype(jnp.bfloat16), dk.reshape(TOKENS, feats).astype(jnp.bfloat16), dv.reshape(TOKENS, feats).astype(jnp.bfloat16), grad_gate, grad_gain)
```

```python
import functools

import jax
import jax.numpy as jnp
from jax import lax
from jax.experimental import pallas as pl
from jax.experimental.pallas import tpu as pltpu
from jax.sharding import PartitionSpec as P

MESH = pl.DeviceIdType.MESH
F32 = jnp.float32
BF16 = jnp.bfloat16
BLOCK = 256
HD = 128
EPS = 1e-06


def nn(a, b):
    return lax.dot_general(a, b, (((1,), (0,)), ((), ())), preferred_element_type=F32)


def nt(a, b):
    return lax.dot_general(a, b, (((1,), (1,)), ((), ())), preferred_element_type=F32)


def tn(a, b):
    return lax.dot_general(a, b, (((0,), (0,)), ((), ())), preferred_element_type=F32)


def drain(ref, count, sem):
    part = ref.at[pl.ds(0, count)]
    pltpu.make_async_copy(part, part, sem).wait()


def kernel(
    dims,
    q_hbm, k_hbm, v_hbm, g_hbm, o_hbm, gain_ref, rate_ref, seg_ref,
    dq_hbm, dk_hbm, dv_hbm, gg_hbm, dgain_ref,
    qv, kv, vv, gv, ov, segc, wl, wf, wb, fst, sw, attn, gs, sst, bc, qwt, datt, rst,
    dkp, dvp, dqv, dkv, dvv, ggv,
    fbuf, rbuf, sbuf, ebuf, fbuf2, rbuf2, sbuf2, ebuf2, lab, flab, rlab, zbuf, gbuf, cbuf,
    in_sem, out_sem, ssem, rsem,
):
    R, Z, RW, N, H = dims
    T = N * BLOCK
    J = R // H
    SR = H * HD // R
    CW = R // RW
    me = lax.axis_index("ctx")
    zme = lax.axis_index("head")
    row0 = (me // RW) * RW
    mcol = me - row0
    mrow = me // RW
    hm = lax.rem(me, H)
    jm = me // H
    myslice = hm * J + jm

    loads = [
        pltpu.make_async_copy(src, dst, in_sem.at[i])
        for i, (src, dst) in enumerate(
            ((k_hbm, kv), (v_hbm, vv), (q_hbm, qv), (g_hbm, gv), (o_hbm, ov))
        )
    ]
    loads[0].start()
    loads[1].start()

    barrier = pltpu.get_barrier_semaphore()

    def greet_ctx(i, c):
        pl.semaphore_signal(
            barrier, inc=1, device_id=(lax.rem(me + i, R), zme), device_id_type=MESH
        )
        return c

    def greet_head(i, c):
        pl.semaphore_signal(
            barrier, inc=1, device_id=(me, lax.rem(zme + i, Z)), device_id_type=MESH
        )
        return c

    lax.fori_loop(1, R, greet_ctx, 0)
    lax.fori_loop(1, Z, greet_head, 0)
    for i in (2, 3, 4):
        loads[i].start()

    def remote(src, dst, phase, ctx, head):
        return pltpu.make_async_remote_copy(
            src_ref=src, dst_ref=dst, send_sem=ssem.at[phase], recv_sem=rsem.at[phase],
            device_id=(ctx, head), device_id_type=MESH,
        )

    def col(h):
        return slice(h * HD, (h + 1) * HD)

    def rows(n):
        start = n * BLOCK
        return pl.ds(start if isinstance(n, int) else pl.multiple_of(start, BLOCK), BLOCK)

    def power(h, times):
        return jnp.exp(jnp.full((1, HD), -rate_ref[h] * times, F32))

    iota = lax.broadcasted_iota(jnp.int32, (BLOCK, HD), 0).astype(F32)
    for h in range(H):
        wl[h] = jnp.exp(-rate_ref[h] * (BLOCK - 1.0 - iota))
    first_row = jnp.where(lax.broadcasted_iota(jnp.int32, (16, HD), 0) == 0, 1.0, 0.0).astype(BF16)
    for n in range(N):
        seg = jnp.broadcast_to(seg_ref[0:1, rows(n)].astype(F32), (16, BLOCK)).astype(BF16)
        segc[rows(n), :] = tn(seg, first_row)
    lab[me] = jnp.concatenate([segc[T - 1 : T, :], segc[0:1, :]], axis=0)
    lam = [power(h, 1.0) for h in range(H)]
    pblock = [power(h, float(BLOCK)) for h in range(H)]

    def scatter_head(h, src, dst, phase):
        def step(i, c):
            j = lax.rem(i + jm, J)
            dest = H * j + h

            @pl.when(dest != me)
            def _():
                remote(src.at[h * J + j], dst.at[me], phase, dest, zme).start()

            return c

        lax.fori_loop(0, J, step, 0)

    loads[0].wait()
    loads[1].wait()
    for h in range(H):
        own = None
        for n in range(N):
            last = segc[n * BLOCK + BLOCK - 1 : n * BLOCK + BLOCK, :]
            here = segc[rows(n), :] == last
            kw = jnp.where(here, kv[rows(n), col(h)].astype(F32) * wl[h], 0.0).astype(BF16)
            f = tn(kw, vv[rows(n), col(h)])
            fst[n, h] = f
            if own is None:
                own = f
            else:
                before = segc[n * BLOCK - 1 : n * BLOCK, :]
                own = jnp.where(before == last, pblock[h], 0.0) * own + f
        fbuf[h * J : (h + 1) * J] = own.reshape(J, SR, HD)
        if h == 0:
            pl.semaphore_wait(barrier, R - 1 + Z - 1)

            def label_row(i, c):
                remote(lab.at[me], lab.at[me], 0, row0 + lax.rem(mcol + i, RW), zme).start()
                return c

            lax.fori_loop(1, RW, label_row, 0)
        scatter_head(h, fbuf, rbuf, 2)
    rbuf[me] = fbuf[myslice]

    drain(lab, RW - 1, rsem.at[0])
    mine = lab.at[pl.ds(row0, RW)]

    def label_col(i, c):
        other = lax.rem(mrow + i, CW)
        remote(mine, mine, 1, other * RW + mcol, zme).start()
        return c

    lax.fori_loop(1, CW, label_col, 0)

    d2 = (
        lax.broadcasted_iota(jnp.int32, (BLOCK, BLOCK), 0)
        - lax.broadcasted_iota(jnp.int32, (BLOCK, BLOCK), 1)
    ).astype(F32)
    for h in range(H):
        wf[h] = jnp.exp(-rate_ref[h] * iota)
        wb[h] = jnp.where(d2 >= 0, jnp.exp(-rate_ref[h] * jnp.maximum(d2, 0.0)), 0.0)

    def same_of(n):
        sc = segc[rows(n), :]
        return jnp.concatenate([sc, sc], axis=1) == seg_ref[0:1, rows(n)].astype(F32)

    def intra(n, c):
        same = same_of(n)
        for h in range(H):
            s = nt(qv[rows(n), col(h)], kv[rows(n), col(h)])
            s = jnp.where(same, s * wb[h], 0.0).astype(BF16)
            sw[n, h] = s
            attn[rows(n), col(h)] = nn(s, vv[rows(n), col(h)])
            sig = jax.nn.sigmoid(gv[rows(n), col(h)].astype(F32))
            gs[rows(n), col(h)] = ov[rows(n), col(h)].astype(F32) * sig
        return c

    for i in (2, 3, 4):
        loads[i].wait()
    lax.fori_loop(0, N // 2, intra, 0)

    def spread(sb, eb, phase):
        def step(i, c):
            dest = lax.rem(me + i, R)
            remote(sb.at[dest], eb.at[myslice], phase, dest, zme).start()
            return c

        lax.fori_loop(1, R, step, 0)
        eb[myslice] = sb[me]

    drain(lab, R - RW, rsem.at[1])
    drain(rbuf, R - 1, rsem.at[2])
    pdev = power(hm, float(T))
    acc = jnp.zeros((SR, HD), F32)
    for r in range(R - 1):
        sbuf[r] = acc
        if r == 0:
            acc = rbuf[r]
        else:
            linked = lab[r - 1, 0:1, :] == lab[r, 0:1, :]
            acc = rbuf[r] + jnp.where(linked, pdev, 0.0) * acc
    sbuf[R - 1] = acc
    spread(sbuf, ebuf, 3)

    lax.fori_loop(N // 2, N, intra, 0)

    flab[0] = lab[jnp.maximum(me - 1, 0), 0:1, :]
    rlab[N - 1] = lab[jnp.minimum(me + 1, R - 1), 1:2, :]
    for n in range(1, N):
        flab[n] = segc[n * BLOCK - 1 : n * BLOCK, :]
        rlab[n - 1] = segc[n * BLOCK : n * BLOCK + 1, :]
    drain(ebuf, R - 1, rsem.at[3])
    for h in range(H):
        state = lam[h] * ebuf[h * J : (h + 1) * J].reshape(HD, HD)
        for n in range(N):
            sst[n, h] = state.astype(BF16)
            if n < N - 1:
                keep = flab[n] == flab[n + 1]
                state = jnp.where(keep, pblock[h], 0.0) * state + lam[h] * fst[n, h]

    row16 = lax.broadcasted_iota(jnp.int32, (16, HD), 0)

    def cross(n, total):
        linked = segc[rows(n), :] == flab[n]
        ssq = jnp.zeros((BLOCK, HD), F32)
        sda = jnp.zeros((BLOCK, HD), F32)
        for h in range(H):
            c = nn(qv[rows(n), col(h)], sst[n, h])
            a = attn[rows(n), col(h)] + jnp.where(linked, wf[h], 0.0) * c
            attn[rows(n), col(h)] = a
            ssq = ssq + a * a
            sda = sda + (gs[rows(n), col(h)] * gain_ref[0:1, col(h)]) * a
        pick1 = jnp.where(row16 == n, 1.0, 0.0).astype(BF16)
        pick2 = jnp.where(row16 == n + N, 1.0, 0.0).astype(BF16)
        return total + nt(pick1, ssq.astype(BF16)) + nt(pick2, sda.astype(BF16))

    total = lax.fori_loop(0, N, cross, jnp.zeros((16, BLOCK), F32))
    zbuf[zme] = total[0 : 2 * N, :]

    def send_head(i, c):
        remote(zbuf.at[zme], zbuf.at[zme], 4, me, lax.rem(zme + i, Z)).start()
        return c

    lax.fori_loop(1, Z, send_head, 0)

    def turn(n, c):
        first = segc[pl.ds(n * BLOCK, 1), :]
        here = segc[rows(n), :] == first
        for h in range(H):
            qw = jnp.where(here, qv[rows(n), col(h)].astype(F32) * wf[h], 0.0)
            qwt[n, h] = qw.T.astype(BF16)
        return c

    lax.fori_loop(0, N, turn, 0)

    drain(zbuf, Z - 1, rsem.at[4])
    tot = zbuf[0]
    for i in range(1, Z):
        tot = tot + zbuf[i]
    feats = float(H * HD * Z)
    rat = lax.rsqrt(tot[0:N] / feats + EPS)
    cor = rat * rat * rat * (tot[N : 2 * N] / feats)
    both = jnp.concatenate([rat, cor], axis=0)
    upper = both.astype(BF16).astype(F32)
    lhs = jnp.concatenate([upper, both - upper], axis=0).astype(BF16)
    wide = 2 * N * HD
    rr = lax.broadcasted_iota(jnp.int32, (4 * N, wide), 0)
    cc = lax.broadcasted_iota(jnp.int32, (4 * N, wide), 1) // HD
    picks = jnp.where((rr == cc) | (rr == cc + 2 * N), 1.0, 0.0).astype(BF16)
    bc[...] = tn(lhs, picks)

    def factor(n):
        if isinstance(n, int):
            return bc[:, n * HD : (n + 1) * HD]
        return bc[:, pl.ds(pl.multiple_of(n * HD, HD), HD)]

    for h in range(H):
        own = None
        for n in reversed(range(N)):
            dz = gs[rows(n), col(h)] * gain_ref[0:1, col(h)]
            d = (factor(n) * dz - factor(N + n) * attn[rows(n), col(h)]).astype(BF16)
            datt[rows(n), col(h)] = d
            f = nn(qwt[n, h], d)
            rst[n, h] = f
            if own is None:
                own = f
            else:
                first = segc[n * BLOCK : n * BLOCK + 1, :]
                after = segc[(n + 1) * BLOCK : (n + 1) * BLOCK + 1, :]
                own = jnp.where(first == after, pblock[h], 0.0) * own + f
        fbuf2[h * J : (h + 1) * J] = own.reshape(J, SR, HD)
        scatter_head(h, fbuf2, rbuf2, 5)
    rbuf2[me] = fbuf2[myslice]

    def gated(n, sums):
        out = []
        for h in range(H):
            normed = attn[rows(n), col(h)] * factor(n)
            t = gs[rows(n), col(h)] * normed
            sig = jax.nn.sigmoid(gv[rows(n), col(h)].astype(F32))
            ggv[rows(n), col(h)] = (t * gain_ref[0:1, col(h)] * (1.0 - sig)).astype(BF16)
            out.append(sums[h] + jnp.sum(t.reshape(BLOCK // 8, 8, HD), axis=0))
        return tuple(out)

    sums = lax.fori_loop(0, N, gated, tuple(jnp.zeros((8, HD), F32) for _ in range(H)))
    gbuf[mcol] = jnp.concatenate([jnp.sum(s, axis=0, keepdims=True) for s in sums], axis=1)
    out_gg = pltpu.make_async_copy(ggv, gg_hbm, out_sem.at[3])
    out_gg.start()

    def gain_row(i, c):
        remote(gbuf.at[mcol], gbuf.at[mcol], 6, row0 + lax.rem(mcol + i, RW), zme).start()
        return c

    lax.fori_loop(1, RW, gain_row, 0)

    def back(n, c):
        same = same_of(n)
        linked = segc[rows(n), :] == flab[n]
        for h in range(H):
            d = datt[rows(n), col(h)]
            s = nt(d, vv[rows(n), col(h)])
            ds = jnp.where(same, s * wb[h], 0.0).astype(BF16)
            dq = nn(ds, kv[rows(n), col(h)])
            dq = dq + jnp.where(linked, wf[h], 0.0) * nt(d, sst[n, h])
            dqv[rows(n), col(h)] = dq.astype(BF16)
            dkp[rows(n), col(h)] = tn(ds, qv[rows(n), col(h)])
            dvp[rows(n), col(h)] = tn(sw[n, h], d)
        return c

    lax.fori_loop(0, N // 2, back, 0)

    drain(rbuf2, R - 1, rsem.at[5])
    acc = jnp.zeros((SR, HD), F32)
    for r in reversed(range(1, R)):
        sbuf2[r] = acc
        if r == R - 1:
            acc = rbuf2[r]
        else:
            linked = lab[r + 1, 1:2, :] == lab[r, 1:2, :]
            acc = rbuf2[r] + jnp.where(linked, pdev, 0.0) * acc
    sbuf2[0] = acc
    spread(sbuf2, ebuf2, 7)

    drain(gbuf, RW - 1, rsem.at[6])
    part = gbuf[0]
    for i in range(1, RW):
        part = part + gbuf[i]
    cbuf[mrow] = part

    def gain_col(i, c):
        other = lax.rem(mrow + i, CW)
        remote(cbuf.at[mrow], cbuf.at[mrow], 8, other * RW + mcol, zme).start()
        return c

    lax.fori_loop(1, CW, gain_col, 0)

    lax.fori_loop(N // 2, N, back, 0)
    out_dq = pltpu.make_async_copy(dqv, dq_hbm, out_sem.at[0])
    out_dq.start()

    drain(ebuf2, R - 1, rsem.at[7])
    states = [lam[h] * ebuf2[h * J : (h + 1) * J].reshape(HD, HD) for h in range(H)]
    outs = []
    for n in reversed(range(N)):
        linked = segc[rows(n), :] == rlab[n]
        for h in range(H):
            rin = states[h].astype(BF16)
            w = jnp.where(linked, wl[h], 0.0)
            dk = dkp[rows(n), col(h)] + w * nt(vv[rows(n), col(h)], rin)
            dv = dvp[rows(n), col(h)] + w * nn(kv[rows(n), col(h)], rin)
            dkv[rows(n), col(h)] = dk.astype(BF16)
            dvv[rows(n), col(h)] = dv.astype(BF16)
            if n > 0:
                keep = rlab[n] == rlab[n - 1]
                states[h] = jnp.where(keep, pblock[h], 0.0) * states[h] + lam[h] * rst[n, h]
        for src, dst, slot in ((dkv, dk_hbm, 4 + n), (dvv, dv_hbm, 4 + N + n)):
            copy = pltpu.make_async_copy(src.at[rows(n)], dst.at[rows(n)], out_sem.at[slot])
            copy.start()
            outs.append(copy)

    drain(cbuf, CW - 1, rsem.at[8])
    part = cbuf[0]
    for i in range(1, CW):
        part = part + cbuf[i]
    dgain_ref[...] = part

    drain(lab, RW - 1, ssem.at[0])
    drain(lab, R - RW, ssem.at[1])
    drain(fbuf, R - 1, ssem.at[2])
    drain(sbuf, R - 1, ssem.at[3])
    drain(zbuf, Z - 1, ssem.at[4])
    drain(fbuf2, R - 1, ssem.at[5])
    drain(gbuf, RW - 1, ssem.at[6])
    drain(sbuf2, R - 1, ssem.at[7])
    drain(cbuf, CW - 1, ssem.at[8])
    out_gg.wait()
    out_dq.wait()
    for copy in outs:
        copy.wait()


def body(queries, keys, values, gate, grad_out, gain, decay_rate, segment_ids):
    R = lax.axis_size("ctx")
    Z = lax.axis_size("head")
    T, W = queries.shape
    H = W // HD
    N = T // BLOCK
    RW = 8 if R == 32 else R // 2
    CW = R // RW
    J = R // H
    SR = H * HD // R
    anyspec = pl.BlockSpec(memory_space=pl.ANY)
    vspec = pl.BlockSpec(memory_space=pltpu.VMEM)
    big = jax.ShapeDtypeStruct((T, W), BF16)
    VM = pltpu.VMEM
    scratch = (
        [VM((T, W), BF16)] * 5
        + [
            VM((T, HD), F32),
            VM((H, BLOCK, HD), F32),
            VM((H, BLOCK, HD), F32),
            VM((H, BLOCK, BLOCK), F32),
            VM((N, H, HD, HD), F32),
            VM((N, H, BLOCK, BLOCK), BF16),
            VM((T, W), F32),
            VM((T, W), F32),
            VM((N, H, HD, HD), BF16),
            VM((BLOCK, 2 * N * HD), F32),
            VM((N, H, HD, BLOCK), BF16),
            VM((T, W), BF16),
            VM((N, H, HD, HD), F32),
            VM((T, W), F32),
            VM((T, W), F32),
        ]
        + [VM((T, W), BF16)] * 4
        + [VM((R, SR, HD), F32)] * 8
        + [
            VM((R, 2, HD), F32),
            VM((N, 1, HD), F32),
            VM((N, 1, HD), F32),
            VM((Z, 2 * N, BLOCK), F32),
            VM((RW, 1, W), F32),
            VM((CW, 1, W), F32),
            pltpu.SemaphoreType.DMA((5,)),
            pltpu.SemaphoreType.DMA((4 + 2 * N,)),
            pltpu.SemaphoreType.DMA((9,)),
            pltpu.SemaphoreType.DMA((9,)),
        ]
    )
    outs = pl.pallas_call(
        functools.partial(kernel, (R, Z, RW, N, H)),
        out_shape=(big, big, big, big, jax.ShapeDtypeStruct((1, W), F32)),
        in_specs=[anyspec] * 5 + [vspec, pl.BlockSpec(memory_space=pltpu.SMEM), vspec],
        out_specs=(anyspec,) * 4 + (vspec,),
        scratch_shapes=scratch,
        compiler_params=pltpu.CompilerParams(
            collective_id=0, has_side_effects=True, vmem_limit_bytes=52 * 1024 * 1024
        ),
    )(
        queries, keys, values, gate, grad_out,
        gain.reshape(1, W), decay_rate, segment_ids.reshape(1, T),
    )
    dq, dk, dv, gg, dgain = outs
    return dq, dk, dv, gg, dgain.reshape(W)


def solution(mesh):
    in_specs = (P("ctx", "head"),) * 5 + (P("head"), P("head"), P("ctx"))
    out_specs = (P("ctx", "head"),) * 4 + (P("head"),)
    return jax.shard_map(body, mesh=mesh, in_specs=in_specs, out_specs=out_specs, check_vma=False)
```

```python
import functools

import jax
import jax.numpy as jnp
from jax import lax
from jax.experimental import pallas as pl
from jax.experimental.pallas import tpu as pltpu
from jax.sharding import PartitionSpec as P

MESH = pl.DeviceIdType.MESH
F32 = jnp.float32
BF16 = jnp.bfloat16
BLOCK = 256
HD = 128
EPS = 1e-06
VMEM_A = 56 * 1024 * 1024


def nn(a, b):
    return lax.dot_general(a, b, (((1,), (0,)), ((), ())), preferred_element_type=F32)


def nt(a, b):
    return lax.dot_general(a, b, (((1,), (1,)), ((), ())), preferred_element_type=F32)


def tn(a, b):
    return lax.dot_general(a, b, (((0,), (0,)), ((), ())), preferred_element_type=F32)


def drain(ref, count, sem):
    part = ref.at[pl.ds(0, count)]
    pltpu.make_async_copy(part, part, sem).wait()


def kernel(
    dims,
    q_hbm, k_hbm, v_hbm, g_hbm, o_hbm, gain_hbm, rate_hbm, seg_hbm,
    dq_hbm, dk_hbm, dv_hbm, gg_hbm, dgain_hbm,
    dqv, dkv, dvv, ggv, dgain_ref, qv, kv, vv, gv, ov, gain_ref, rate_ref, seg_ref,
    segc, wl, wf, wb, fst, sw, attn, gs, sst, bc, qwt, datt, rst, dkp, dvp, ssq, sda,
    pbs0, pbr0, hfs, fen, fbuf0, rbuf0, sbuf0, ebuf0, qbs0, qbr0,
    pbs1, pbr1, fen1, fbuf1, rbuf1, sbuf1, ebuf1, qbs1, qbr1,
    flab, rlab, zbuf, gbuf, cbuf,
    in_sem, out_sem, ssem, rsem,
):
    R, Z, RW, N, H = dims
    T = N * BLOCK
    C = R // 2
    HH = H // 2
    HR = HH * HD
    SR = HR // C
    HJ = C // HH
    CW = R // RW
    CX = 4
    CY = C // CX
    me = lax.axis_index("ctx")
    zme = lax.axis_index("head")
    row0 = (me // RW) * RW
    mcol = me - row0
    mrow = me // RW
    core = lax.rem(me, 2)
    mate = me + 1 - 2 * core
    chip = me // 2
    chipy = chip // CX
    chipx = lax.rem(chip, CX)
    own0 = HH * core
    other0 = HH * (1 - core)

    loads = [
        pltpu.make_async_copy(src, dst, in_sem.at[i])
        for i, (src, dst) in enumerate(
            (
                (seg_hbm, seg_ref), (rate_hbm, rate_ref), (k_hbm, kv), (v_hbm, vv),
                (q_hbm, qv), (g_hbm, gv), (o_hbm, ov), (gain_hbm, gain_ref),
            )
        )
    ]
    for copy in loads[:4]:
        copy.start()

    barrier = pltpu.get_barrier_semaphore()

    def greet(ctx, head):
        pl.semaphore_signal(barrier, inc=1, device_id=(ctx, head), device_id_type=MESH)

    def greet_ctx(i, c):
        greet(lax.rem(me + i, R), zme)
        return c

    def greet_head(i, c):
        greet(me, lax.rem(zme + i, Z))
        return c

    lax.fori_loop(1, Z, greet_head, 0)
    lax.fori_loop(1, R, greet_ctx, 0)
    for copy in loads[4:]:
        copy.start()

    def remote(src, dst, phase, ctx, head):
        return pltpu.make_async_remote_copy(
            src_ref=src, dst_ref=dst, send_sem=ssem.at[phase], recv_sem=rsem.at[phase],
            device_id=(ctx, head), device_id_type=MESH,
        )

    def col(h):
        start = h * HD
        return pl.ds(start if isinstance(h, int) else pl.multiple_of(start, HD), HD)

    def rows(n):
        start = n * BLOCK
        return pl.ds(start if isinstance(n, int) else pl.multiple_of(start, BLOCK), BLOCK)

    def power(h, times):
        return jnp.exp(jnp.full((1, HD), -rate_ref[h] * times, F32))

    iota = lax.broadcasted_iota(jnp.int32, (BLOCK, HD), 0).astype(F32)
    first_row = jnp.where(lax.broadcasted_iota(jnp.int32, (16, HD), 0) == 0, 1.0, 0.0).astype(BF16)
    loads[0].wait()
    for n in range(N):
        seg = jnp.broadcast_to(seg_ref[0:1, rows(n)].astype(F32), (16, BLOCK)).astype(BF16)
        segc[rows(n), :] = tn(seg, first_row)
    loads[1].wait()
    for h in range(H):
        wl[h] = jnp.exp(-rate_ref[h] * (BLOCK - 1.0 - iota))
    mylast = segc[T - 1 : T, :]
    myfirst = segc[0:1, :]

    def reach(o):
        return min(o[0], CY - o[0]) + min(o[1], CX - o[1])

    offsets = sorted(
        ((dy, dx) for dy in range(CY) for dx in range(CX) if dy or dx), key=reach, reverse=True
    )

    def each_chip(send):
        for dy, dx in offsets:
            send(lax.rem(chipy + dy, CY) * CX + lax.rem(chipx + dx, CX))

    def merge(entry, pbr, lab_m, lab_p, fen_ref, fbuf):
        is_entry = core == entry
        lab_entry = lax.select(is_entry, lab_m, lab_p)
        lab_exit = lax.select(is_entry, lab_p, lab_m)
        for i in range(HH):
            part = slice(i * HD, (i + 1) * HD)
            fm = hfs[part, :]
            fp = pbr[part, :]
            fe = lax.select(is_entry, fm, fp)
            fx = lax.select(is_entry, fp, fm)
            fen_ref[part, :] = fe
            c = fx + jnp.where(lab_entry == lab_exit, power(own0 + i, float(T)), 0.0) * fe
            fbuf[i * HJ : (i + 1) * HJ, 0:SR, :] = c.reshape(HJ, SR, HD)
        return lab_entry, lab_exit

    def hand_over(entry, fen_ref, ebuf, lab_entry, lab_in, qbs):
        is_entry = core == entry
        kept = []
        for i in range(HH):
            part = slice(i * HD, (i + 1) * HD)
            ve = ebuf[i * HJ : (i + 1) * HJ].reshape(HD, HD)
            linked = jnp.where(lab_in == lab_entry, power(own0 + i, float(T)), 0.0)
            vx = fen_ref[part, :] + linked * ve
            qbs[part, :] = lax.select(is_entry, vx, ve)
            kept.append(lax.select(is_entry, ve, vx))
        return kept, lax.select(is_entry, lab_in, lab_entry)

    def device_state(h):
        own = None
        pb = power(h, float(BLOCK))
        w = wl[h]
        for n in range(N):
            last = segc[n * BLOCK + BLOCK - 1 : n * BLOCK + BLOCK, :]
            here = segc[rows(n), :] == last
            kw = jnp.where(here, kv[rows(n), col(h)].astype(F32) * w, 0.0).astype(BF16)
            f = tn(kw, vv[rows(n), col(h)])
            fst[n, h] = f
            if own is None:
                own = f
            else:
                before = segc[n * BLOCK - 1 : n * BLOCK, :]
                own = jnp.where(before == last, pb, 0.0) * own + f
        return own

    loads[2].wait()
    loads[3].wait()
    for i in range(HH):
        pbs0[i * HD : (i + 1) * HD, :] = device_state(other0 + i)
    top = lax.broadcasted_iota(jnp.int32, (8, HD), 0) == 0
    pbs0[HR : HR + 8, :] = jnp.where(top, mylast, myfirst)
    pl.semaphore_wait(barrier, R - 1 + Z - 1)
    pair0 = remote(pbs0, pbr0, 0, mate, zme)
    pair0.start()
    for i in range(HH):
        hfs[i * HD : (i + 1) * HD, :] = device_state(own0 + i)
    pair0.wait_recv()
    matelast = pbr0[HR : HR + 1, :]
    matefirst = pbr0[HR + 1 : HR + 2, :]
    lab_entry0, lab_exit0 = merge(0, pbr0, mylast, matelast, fen, fbuf0)
    chipfirst = lax.select(core == 0, myfirst, matefirst)
    for c in range(C):
        fbuf0[c, SR : SR + 2, :] = jnp.concatenate([lab_exit0, chipfirst], axis=0)

    def scatter(fbuf, rbuf, phase):
        def send(c):
            remote(fbuf.at[c], rbuf.at[chip], phase, 2 * c + core, zme).start()

        each_chip(send)
        rbuf[chip] = fbuf[chip]

    def spread(sbuf, ebuf, phase):
        def send(c):
            remote(sbuf.at[c], ebuf.at[chip], phase, 2 * c + core, zme).start()

        each_chip(send)
        ebuf[chip] = sbuf[chip]

    scatter(fbuf0, rbuf0, 1)

    d2 = (
        lax.broadcasted_iota(jnp.int32, (BLOCK, BLOCK), 0)
        - lax.broadcasted_iota(jnp.int32, (BLOCK, BLOCK), 1)
    ).astype(F32)
    for h in range(H):
        wf[h] = jnp.exp(-rate_ref[h] * iota)
        wb[h] = jnp.where(d2 >= 0, jnp.exp(-rate_ref[h] * jnp.maximum(d2, 0.0)), 0.0)

    def same_of(n):
        sc = segc[rows(n), :]
        return jnp.concatenate([sc, sc], axis=1) == seg_ref[0:1, rows(n)].astype(F32)

    def intra(n, c):
        same = same_of(n)
        for h in range(H):
            s = nt(qv[rows(n), col(h)], kv[rows(n), col(h)])
            s = jnp.where(same, s * wb[h], 0.0).astype(BF16)
            sw[n, h] = s
            attn[rows(n), col(h)] = nn(s, vv[rows(n), col(h)])
            sig = jax.nn.sigmoid(gv[rows(n), col(h)].astype(F32))
            gs[rows(n), col(h)] = ov[rows(n), col(h)].astype(F32) * sig
        return c

    for copy in loads[4:]:
        copy.wait()
    lax.fori_loop(0, N // 2, intra, 0)

    hold = own0 + chip // HJ
    pchip = power(hold, 2.0 * T)
    drain(rbuf0, C - 1, rsem.at[1])
    acc = jnp.zeros((SR, HD), F32)
    for c in range(C - 1):
        sbuf0[c] = acc
        if c == 0:
            acc = rbuf0[c, 0:SR, :]
        else:
            linked = rbuf0[c - 1, SR : SR + 1, :] == rbuf0[c, SR : SR + 1, :]
            acc = rbuf0[c, 0:SR, :] + jnp.where(linked, pchip, 0.0) * acc
    sbuf0[C - 1] = acc
    spread(sbuf0, ebuf0, 2)

    lax.fori_loop(N // 2, N, intra, 0)

    def chain(h, incoming):
        lam = power(h, 1.0)
        pb = power(h, float(BLOCK))
        state = lam * incoming
        for n in range(N):
            sst[n, h] = state.astype(BF16)
            if n < N - 1:
                keep = flab[n] == flab[n + 1]
                state = jnp.where(keep, pb, 0.0) * state + lam * fst[n, h]

    row16 = lax.broadcasted_iota(jnp.int32, (16, HD), 0)

    def cross(n, h0):
        linked = segc[rows(n), :] == flab[n]
        sq = jnp.zeros((BLOCK, HD), F32)
        da = jnp.zeros((BLOCK, HD), F32)
        for i in range(HH):
            h = h0 + i
            c = nn(qv[rows(n), col(h)], sst[n, h])
            a = attn[rows(n), col(h)] + jnp.where(linked, wf[h], 0.0) * c
            attn[rows(n), col(h)] = a
            sq = sq + a * a
            da = da + (gs[rows(n), col(h)] * gain_ref[0:1, col(h)]) * a
        return sq, da

    def cross_own(n, c):
        sq, da = cross(n, own0)
        ssq[rows(n), :] = sq
        sda[rows(n), :] = da
        return c

    def cross_other(n, total):
        sq, da = cross(n, other0)
        pick1 = jnp.where(row16 == n, 1.0, 0.0).astype(BF16)
        pick2 = jnp.where(row16 == n + N, 1.0, 0.0).astype(BF16)
        sq = (sq + ssq[rows(n), :]).astype(BF16)
        da = (da + sda[rows(n), :]).astype(BF16)
        return total + nt(pick1, sq) + nt(pick2, da)

    lab_in0 = rbuf0[jnp.maximum(chip - 1, 0), SR : SR + 1, :]
    for n in range(1, N):
        flab[n] = segc[n * BLOCK - 1 : n * BLOCK, :]
        rlab[n - 1] = segc[n * BLOCK : n * BLOCK + 1, :]
    drain(ebuf0, C - 1, rsem.at[2])
    kept, label = hand_over(0, fen, ebuf0, lab_entry0, lab_in0, qbs0)
    flab[0] = label
    post0 = remote(qbs0, qbr0, 3, mate, zme)
    post0.start()
    for i in range(HH):
        chain(own0 + i, kept[i])
    lax.fori_loop(0, N, cross_own, 0)
    post0.wait_recv()
    for i in range(HH):
        chain(other0 + i, qbr0[i * HD : (i + 1) * HD, :])
    total = lax.fori_loop(0, N, cross_other, jnp.zeros((16, BLOCK), F32))
    zbuf[zme] = total[0 : 2 * N, :]

    zorder = sorted(range(1, Z), key=lambda i: min(i, Z - i), reverse=True)
    for i in zorder:
        remote(zbuf.at[zme], zbuf.at[zme], 4, me, lax.rem(zme + i, Z)).start()

    def turn(n, c):
        first = segc[pl.ds(n * BLOCK, 1), :]
        here = segc[rows(n), :] == first
        for h in range(H):
            qw = jnp.where(here, qv[rows(n), col(h)].astype(F32) * wf[h], 0.0)
            qwt[n, h] = qw.T.astype(BF16)
        return c

    lax.fori_loop(0, N, turn, 0)

    feats = float(H * HD * Z)
    wide = 2 * N * HD
    rr = lax.broadcasted_iota(jnp.int32, (4 * N, wide), 0)
    cc = lax.broadcasted_iota(jnp.int32, (4 * N, wide), 1) // HD
    picks = jnp.where((rr == cc) | (rr == cc + 2 * N), 1.0, 0.0).astype(BF16)
    drain(zbuf, Z - 1, rsem.at[4])
    tot = zbuf[0]
    for i in range(1, Z):
        tot = tot + zbuf[i]
    rat = lax.rsqrt(tot[0:N] / feats + EPS)
    cor = rat * rat * rat * (tot[N : 2 * N] / feats)
    both = jnp.concatenate([rat, cor], axis=0)
    upper = both.astype(BF16).astype(F32)
    lhs = jnp.concatenate([upper, both - upper], axis=0).astype(BF16)
    bc[...] = tn(lhs, picks)

    def factor(n):
        if isinstance(n, int):
            return bc[:, n * HD : (n + 1) * HD]
        return bc[:, pl.ds(pl.multiple_of(n * HD, HD), HD)]

    def reverse_state(h):
        own = None
        pb = power(h, float(BLOCK))
        for n in reversed(range(N)):
            dz = gs[rows(n), col(h)] * gain_ref[0:1, col(h)]
            d = (factor(n) * dz - factor(N + n) * attn[rows(n), col(h)]).astype(BF16)
            datt[rows(n), col(h)] = d
            f = nn(qwt[n, h], d)
            rst[n, h] = f
            if own is None:
                own = f
            else:
                first = segc[n * BLOCK : n * BLOCK + 1, :]
                after = segc[(n + 1) * BLOCK : (n + 1) * BLOCK + 1, :]
                own = jnp.where(first == after, pb, 0.0) * own + f
        return own

    for i in range(HH):
        pbs1[i * HD : (i + 1) * HD, :] = reverse_state(other0 + i)
    pair1 = remote(pbs1, pbr1, 5, mate, zme)
    pair1.start()
    for i in range(HH):
        hfs[i * HD : (i + 1) * HD, :] = reverse_state(own0 + i)
    pair1.wait_recv()
    lab_entry1, _ = merge(1, pbr1, myfirst, matefirst, fen1, fbuf1)
    scatter(fbuf1, rbuf1, 6)

    def gated(n, sums):
        out = []
        for h in range(H):
            normed = attn[rows(n), col(h)] * factor(n)
            t = gs[rows(n), col(h)] * normed
            sig = jax.nn.sigmoid(gv[rows(n), col(h)].astype(F32))
            ggv[rows(n), col(h)] = (t * gain_ref[0:1, col(h)] * (1.0 - sig)).astype(BF16)
            out.append(sums[h] + jnp.sum(t.reshape(BLOCK // 8, 8, HD), axis=0))
        return tuple(out)

    sums = lax.fori_loop(0, N, gated, tuple(jnp.zeros((8, HD), F32) for _ in range(H)))
    gbuf[mcol] = jnp.concatenate([jnp.sum(s, axis=0, keepdims=True) for s in sums], axis=1)

    def gain_row(i, c):
        remote(gbuf.at[mcol], gbuf.at[mcol], 7, row0 + lax.rem(mcol + i, RW), zme).start()
        return c

    lax.fori_loop(1, RW, gain_row, 0)
    out_gg = pltpu.make_async_copy(ggv, gg_hbm, out_sem.at[0])
    out_gg.start()

    def back(n, c):
        same = same_of(n)
        linked = segc[rows(n), :] == flab[n]
        for h in range(H):
            d = datt[rows(n), col(h)]
            s = nt(d, vv[rows(n), col(h)])
            ds = jnp.where(same, s * wb[h], 0.0).astype(BF16)
            dq = nn(ds, kv[rows(n), col(h)])
            dq = dq + jnp.where(linked, wf[h], 0.0) * nt(d, sst[n, h])
            dqv[rows(n), col(h)] = dq.astype(BF16)
            dkp[rows(n), col(h)] = tn(ds, qv[rows(n), col(h)])
            dvp[rows(n), col(h)] = tn(sw[n, h], d)
        return c

    lax.fori_loop(0, N // 2, back, 0)

    drain(rbuf1, C - 1, rsem.at[6])
    acc = jnp.zeros((SR, HD), F32)
    for c in reversed(range(1, C)):
        sbuf1[c] = acc
        if c == C - 1:
            acc = rbuf1[c]
        else:
            linked = rbuf0[c + 1, SR + 1 : SR + 2, :] == rbuf0[c, SR + 1 : SR + 2, :]
            acc = rbuf1[c] + jnp.where(linked, pchip, 0.0) * acc
    sbuf1[0] = acc
    spread(sbuf1, ebuf1, 8)

    drain(gbuf, RW - 1, rsem.at[7])
    part = gbuf[0]
    for i in range(1, RW):
        part = part + gbuf[i]
    cbuf[mrow] = part

    def gain_col(i, c):
        other = lax.rem(mrow + i, CW)
        remote(cbuf.at[mrow], cbuf.at[mrow], 9, other * RW + mcol, zme).start()
        return c

    lax.fori_loop(1, CW, gain_col, 0)

    lax.fori_loop(N // 2, N, back, 0)
    out_dq = pltpu.make_async_copy(dqv, dq_hbm, out_sem.at[1])
    out_dq.start()

    drain(cbuf, CW - 1, rsem.at[9])
    part = cbuf[0]
    for i in range(1, CW):
        part = part + cbuf[i]
    dgain_ref[...] = part
    out_gain = pltpu.make_async_copy(dgain_ref, dgain_hbm, out_sem.at[2])
    out_gain.start()

    def finish(h, incoming):
        lam = power(h, 1.0)
        pb = power(h, float(BLOCK))
        state = lam * incoming
        for n in reversed(range(N)):
            rin = state.astype(BF16)
            w = jnp.where(segc[rows(n), :] == rlab[n], wl[h], 0.0)
            dk = dkp[rows(n), col(h)] + w * nt(vv[rows(n), col(h)], rin)
            dv = dvp[rows(n), col(h)] + w * nn(kv[rows(n), col(h)], rin)
            dkv[rows(n), col(h)] = dk.astype(BF16)
            dvv[rows(n), col(h)] = dv.astype(BF16)
            if n > 0:
                keep = rlab[n] == rlab[n - 1]
                state = jnp.where(keep, pb, 0.0) * state + lam * rst[n, h]

    lab_in1 = rbuf0[jnp.minimum(chip + 1, C - 1), SR + 1 : SR + 2, :]
    drain(ebuf1, C - 1, rsem.at[8])
    kept, label = hand_over(1, fen1, ebuf1, lab_entry1, lab_in1, qbs1)
    rlab[N - 1] = label
    post1 = remote(qbs1, qbr1, 10, mate, zme)
    post1.start()
    outs = [out_gg, out_dq, out_gain]

    def put(h0, slot):
        part = pl.ds(pl.multiple_of(h0 * HD, HD), HH * HD)
        for i, (src, dst) in enumerate(((dkv, dk_hbm), (dvv, dv_hbm))):
            copy = pltpu.make_async_copy(src.at[:, part], dst.at[:, part], out_sem.at[slot + i])
            copy.start()
            outs.append(copy)

    for i in range(HH):
        finish(own0 + i, kept[i])
    put(own0, 3)
    post1.wait_recv()
    for i in range(HH):
        finish(other0 + i, qbr1[i * HD : (i + 1) * HD, :])
    put(other0, 5)
    for copy in outs:
        copy.wait()

    for copy in (pair0, post0, pair1, post1):
        copy.wait_send()
    drain(fbuf0, C - 1, ssem.at[1])
    drain(sbuf0, C - 1, ssem.at[2])
    drain(zbuf, Z - 1, ssem.at[4])
    drain(fbuf1, C - 1, ssem.at[6])
    drain(gbuf, RW - 1, ssem.at[7])
    drain(sbuf1, C - 1, ssem.at[8])
    drain(cbuf, CW - 1, ssem.at[9])


def mover(parts, *refs):
    half = len(parts)
    srcs, dsts, held = refs[:half], refs[half : 2 * half], refs[2 * half : 3 * half]
    sin, sout = refs[3 * half :]
    ins, outs = [], []
    for i in range(half):
        step = srcs[i].shape[0] // parts[i]
        for j in range(parts[i]):
            piece = pl.ds(j * step, step)
            slot = len(ins)
            ins.append(pltpu.make_async_copy(srcs[i].at[piece], held[i].at[piece], sin.at[slot]))
            outs.append(pltpu.make_async_copy(held[i].at[piece], dsts[i].at[piece], sout.at[slot]))
    for copy in ins:
        copy.start()
    for a, b in zip(ins, outs):
        a.wait()
        b.start()
    for copy in outs:
        copy.wait()


def body(queries, keys, values, gate, grad_out, gain, decay_rate, segment_ids):
    R = lax.axis_size("ctx")
    Z = lax.axis_size("head")
    T, W = queries.shape
    H = W // HD
    N = T // BLOCK
    RW = 8 if R == 32 else R // 2
    CW = R // RW
    C = R // 2
    HR = H * HD // 2
    SR = HR // C
    hbm = pl.BlockSpec(memory_space=pltpu.HBM)
    big = jax.ShapeDtypeStruct((T, W), BF16)
    small = jax.ShapeDtypeStruct((1, W), F32)
    VM = pltpu.VMEM
    scratch = (
        [VM((T, W), BF16)] * 4
        + [VM((1, W), F32)]
        + [VM((T, W), BF16)] * 5
        + [VM((1, W), F32), pltpu.SMEM((H,), F32), VM((1, T), jnp.int32)]
        + [
            VM((T, HD), F32),
            VM((H, BLOCK, HD), F32),
            VM((H, BLOCK, HD), F32),
            VM((H, BLOCK, BLOCK), F32),
            VM((N, H, HD, HD), F32),
            VM((N, H, BLOCK, BLOCK), BF16),
            VM((T, W), F32),
            VM((T, W), F32),
            VM((N, H, HD, HD), BF16),
            VM((BLOCK, 2 * N * HD), F32),
            VM((N, H, HD, BLOCK), BF16),
            VM((T, W), BF16),
            VM((N, H, HD, HD), F32),
            VM((T, W), F32),
            VM((T, W), F32),
            VM((T, HD), F32),
            VM((T, HD), F32),
        ]
        + [VM((HR + 8, HD), F32)] * 2
        + [VM((HR, HD), F32)] * 2
        + [VM((C, SR + 2, HD), F32)] * 2
        + [VM((C, SR, HD), F32)] * 2
        + [VM((HR, HD), F32)] * 2
        + [VM((HR, HD), F32)] * 3
        + [VM((C, SR, HD), F32)] * 4
        + [VM((HR, HD), F32)] * 2
        + [
            VM((N, 1, HD), F32),
            VM((N, 1, HD), F32),
            VM((Z, 2 * N, BLOCK), F32),
            VM((RW, 1, W), F32),
            VM((CW, 1, W), F32),
            pltpu.SemaphoreType.DMA((8,)),
            pltpu.SemaphoreType.DMA((7,)),
            pltpu.SemaphoreType.DMA((11,)),
            pltpu.SemaphoreType.DMA((11,)),
        ]
    )
    outs = pl.pallas_call(
        functools.partial(kernel, (R, Z, RW, N, H)),
        out_shape=(big, big, big, big, small),
        in_specs=[hbm] * 8,
        out_specs=(hbm,) * 5,
        scratch_shapes=scratch,
        compiler_params=pltpu.CompilerParams(
            collective_id=0, has_side_effects=True, vmem_limit_bytes=VMEM_A
        ),
    )(
        queries, keys, values, gate, grad_out,
        gain.reshape(1, W), decay_rate, segment_ids.reshape(1, T),
    )
    parts = (2, 2, 2, 2, 1)
    moved = pl.pallas_call(
        functools.partial(mover, parts),
        out_shape=(big, big, big, big, small),
        in_specs=[hbm] * 5,
        out_specs=(hbm,) * 5,
        scratch_shapes=[VM((T, W), BF16)] * 4
        + [VM((1, W), F32)]
        + [pltpu.SemaphoreType.DMA((sum(parts),))] * 2,
        compiler_params=pltpu.CompilerParams(vmem_limit_bytes=VMEM_A),
    )(*outs)
    dq, dk, dv, gg, dgain = moved
    return dq, dk, dv, gg, dgain.reshape(W)


def solution(mesh):
    in_specs = (P("ctx", "head"),) * 5 + (P("head"), P("head"), P("ctx"))
    out_specs = (P("ctx", "head"),) * 4 + (P("head"),)
    return jax.shard_map(body, mesh=mesh, in_specs=in_specs, out_specs=out_specs, check_vma=False)
```

```python
import functools

import jax
import jax.numpy as jnp
from jax import lax
from jax.experimental import pallas as pl
from jax.experimental.pallas import tpu as pltpu
from jax.sharding import PartitionSpec as P

MESH = pl.DeviceIdType.MESH
F32 = jnp.float32
BF16 = jnp.bfloat16
BLOCK = 256
HD = 128
EPS = 1e-06
VMEM_A = 49 * 1024 * 1024
VMEM_B = 8 * 1024 * 1024


def nn(a, b):
    return lax.dot_general(a, b, (((1,), (0,)), ((), ())), preferred_element_type=F32)


def nt(a, b):
    return lax.dot_general(a, b, (((1,), (1,)), ((), ())), preferred_element_type=F32)


def tn(a, b):
    return lax.dot_general(a, b, (((0,), (0,)), ((), ())), preferred_element_type=F32)


def drain(ref, count, sem):
    if count == 0:
        return
    part = ref.at[pl.ds(0, count)]
    pltpu.make_async_copy(part, part, sem).wait()


def kernel(
    dims,
    q_hbm, k_hbm, v_hbm, g_hbm, o_hbm, gain_hbm, rate_hbm, seg_hbm,
    dqv, dkv, dvv, ggv, dgain_ref,
    qv, kv, vv, gv, ov, gain_ref, rate_ref, seg_ref,
    segc, wl, wf, wb, fst, sw, attn, dzs, sst, bc, qwt, datt, rst, dkp, dvp, ssq, sda, qc, pows,
    pbs0, pbr0, hfs, fen, fbuf0, rbuf0, sbuf0, ebuf0, qbs0, qbr0,
    pbs1, pbr1, fen1, fbuf1, rbuf1, sbuf1, ebuf1, qbs1, qbr1,
    flab, rlab, zbuf, gbuf, cbuf,
    in_sem, ssem, rsem,
):
    R, Z, RW, N, H = dims
    T = N * BLOCK
    C = R // 2
    HH = H // 2
    HR = HH * HD
    CX = 4
    SR = HR // CX
    HJ = CX // HH
    CW = R // RW
    CY = C // CX
    me = lax.axis_index("ctx")
    zme = lax.axis_index("head")
    row0 = (me // RW) * RW
    mcol = me - row0
    mrow = me // RW
    core = lax.rem(me, 2)
    mate = me + 1 - 2 * core
    chip = me // 2
    chipy = chip // CX
    chipx = lax.rem(chip, CX)
    own0 = HH * core
    other0 = HH * (1 - core)

    loads = [
        pltpu.make_async_copy(src, dst, in_sem.at[i])
        for i, (src, dst) in enumerate(
            (
                (seg_hbm, seg_ref), (rate_hbm, rate_ref), (k_hbm, kv), (v_hbm, vv),
                (q_hbm, qv), (g_hbm, gv), (o_hbm, ov), (gain_hbm, gain_ref),
            )
        )
    ]
    for copy in loads[:4]:
        copy.start()

    barrier = pltpu.get_barrier_semaphore()

    def greet(ctx, head):
        pl.semaphore_signal(barrier, inc=1, device_id=(ctx, head), device_id_type=MESH)

    def greet_ctx(i, c):
        greet(lax.rem(me + i, R), zme)
        return c

    def greet_head(i, c):
        greet(me, lax.rem(zme + i, Z))
        return c

    lax.fori_loop(1, Z, greet_head, 0)
    lax.fori_loop(1, R, greet_ctx, 0)
    for copy in loads[4:]:
        copy.start()

    def remote(src, dst, phase, ctx, head):
        return pltpu.make_async_remote_copy(
            src_ref=src, dst_ref=dst, send_sem=ssem.at[phase], recv_sem=rsem.at[phase],
            device_id=(ctx, head), device_id_type=MESH,
        )

    def col(h):
        start = h * HD
        return pl.ds(start if isinstance(h, int) else pl.multiple_of(start, HD), HD)

    def rows(n):
        start = n * BLOCK
        return pl.ds(start if isinstance(n, int) else pl.multiple_of(start, BLOCK), BLOCK)

    def power(h, times):
        return jnp.exp(jnp.full((1, HD), -rate_ref[h] * times, F32))

    iota = lax.broadcasted_iota(jnp.int32, (BLOCK, HD), 0).astype(F32)
    first_row = jnp.where(lax.broadcasted_iota(jnp.int32, (16, HD), 0) == 0, 1.0, 0.0).astype(BF16)
    loads[0].wait()
    for n in range(N):
        seg = jnp.broadcast_to(seg_ref[0:1, rows(n)].astype(F32), (16, BLOCK)).astype(BF16)
        segc[rows(n), :] = tn(seg, first_row)
    loads[1].wait()
    for h in range(H):
        wl[h] = jnp.exp(-rate_ref[h] * (BLOCK - 1.0 - iota))
        for i, times in enumerate((1.0, float(BLOCK), float(T), 2.0 * T)):
            pows[i, h] = power(h, times)
    mylast = segc[T - 1 : T, :]
    myfirst = segc[0:1, :]

    def at_chip(y, x):
        return 2 * (y * CX + x) + core

    around = (2, 1, 3)

    def merge(entry, pbr, lab_m, lab_p, fen_ref, fbuf):
        is_entry = core == entry
        lab_entry = lax.select(is_entry, lab_m, lab_p)
        lab_exit = lax.select(is_entry, lab_p, lab_m)
        for i in range(HH):
            part = slice(i * HD, (i + 1) * HD)
            fm = hfs[part, :]
            fp = pbr[part, :]
            fe = lax.select(is_entry, fm, fp)
            fx = lax.select(is_entry, fp, fm)
            fen_ref[part, :] = fe
            c = fx + jnp.where(lab_entry == lab_exit, pows[2, own0 + i], 0.0) * fe
            fbuf[i * HJ : (i + 1) * HJ, 0:SR, :] = c.reshape(HJ, SR, HD)
        return lab_entry, lab_exit

    def hand_over(entry, fen_ref, ebuf, lab_entry, lab_in, qbs):
        is_entry = core == entry
        kept = []
        for i in range(HH):
            part = slice(i * HD, (i + 1) * HD)
            ve = ebuf[i * HJ : (i + 1) * HJ].reshape(HD, HD)
            linked = jnp.where(lab_in == lab_entry, pows[2, own0 + i], 0.0)
            vx = fen_ref[part, :] + linked * ve
            qbs[part, :] = lax.select(is_entry, vx, ve)
            kept.append(lax.select(is_entry, ve, vx))
        return kept

    def device_state(h):
        own = None
        pb = pows[1, h]
        w = wl[h]
        for n in range(N):
            last = segc[n * BLOCK + BLOCK - 1 : n * BLOCK + BLOCK, :]
            here = segc[rows(n), :] == last
            kw = jnp.where(here, kv[rows(n), col(h)].astype(F32) * w, 0.0).astype(BF16)
            f = tn(kw, vv[rows(n), col(h)])
            fst[n, h] = f
            if own is None:
                own = f
            else:
                before = segc[n * BLOCK - 1 : n * BLOCK, :]
                own = jnp.where(before == last, pb, 0.0) * own + f
        return own

    loads[2].wait()
    loads[3].wait()
    for i in range(HH):
        pbs0[i * HD : (i + 1) * HD, :] = device_state(other0 + i)
    top = lax.broadcasted_iota(jnp.int32, (8, HD), 0) == 0
    pbs0[HR : HR + 8, :] = jnp.where(top, mylast, myfirst)
    pl.semaphore_wait(barrier, R - 1 + Z - 1)
    pair0 = remote(pbs0, pbr0, 0, mate, zme)
    pair0.start()
    for i in range(HH):
        hfs[i * HD : (i + 1) * HD, :] = device_state(own0 + i)
    pair0.wait_recv()
    matelast = pbr0[HR : HR + 1, :]
    matefirst = pbr0[HR + 1 : HR + 2, :]
    lab_entry0, lab_exit0 = merge(0, pbr0, mylast, matelast, fen, fbuf0)
    for x in range(CX):
        fbuf0[x, SR : SR + 1, :] = lab_exit0

    def scatter(fbuf, rbuf, phase, turn_y, near, far):
        there = lax.rem(chipy + turn_y, CY)
        for dx in (2, 1, 3, 0):
            x = lax.rem(chipx + dx, CX)
            remote(fbuf.at[x], rbuf.at[far + chipx], phase, at_chip(there, x), zme).start()
        for dx in around:
            x = lax.rem(chipx + dx, CX)
            remote(fbuf.at[x], rbuf.at[near + chipx], phase, at_chip(chipy, x), zme).start()
        rbuf[near + chipx] = fbuf[chipx]

    def spread(sbuf, ebuf, phase):
        for dx in around:
            x = lax.rem(chipx + dx, CX)
            remote(sbuf.at[x], ebuf.at[chipx], phase, at_chip(chipy, x), zme).start()
        ebuf[chipx] = sbuf[chipx]

    scatter(fbuf0, rbuf0, 1, 1, CX, 0)

    d2 = (
        lax.broadcasted_iota(jnp.int32, (BLOCK, BLOCK), 0)
        - lax.broadcasted_iota(jnp.int32, (BLOCK, BLOCK), 1)
    ).astype(F32)
    for h in range(H):
        wf[h] = jnp.exp(-rate_ref[h] * iota)
        wb[h] = jnp.where(d2 >= 0, jnp.exp(-rate_ref[h] * jnp.maximum(d2, 0.0)), 0.0)

    def same_of(n):
        sc = segc[rows(n), :]
        return jnp.concatenate([sc, sc], axis=1) == seg_ref[0:1, rows(n)].astype(F32)

    def intra(n, c):
        same = same_of(n)
        for h in range(H):
            s = nt(qv[rows(n), col(h)], kv[rows(n), col(h)])
            s = jnp.where(same, s * wb[h], 0.0).astype(BF16)
            sw[n, h] = s
            attn[rows(n), col(h)] = nn(s, vv[rows(n), col(h)])
            sig = jax.nn.sigmoid(gv[rows(n), col(h)].astype(F32))
            dzs[rows(n), col(h)] = ov[rows(n), col(h)].astype(F32) * sig * gain_ref[0:1, col(h)]
        return c

    for copy in loads[4:]:
        copy.wait()
    lax.fori_loop(0, N // 2, intra, 0)

    pchip = pows[3, own0 + chipx // HJ]
    drain(rbuf0, 2 * CX - 1, rsem.at[1])
    acc = rbuf0[0, 0:SR, :]
    for i in range(1, 2 * CX):
        if i >= CX:
            sbuf0[i - CX] = acc
        if i < 2 * CX - 1:
            linked = rbuf0[i - 1, SR : SR + 1, :] == rbuf0[i, SR : SR + 1, :]
            acc = rbuf0[i, 0:SR, :] + jnp.where(linked, pchip, 0.0) * acc
    spread(sbuf0, ebuf0, 2)

    lab_in0 = rbuf0[CX - 1 + chipx, SR : SR + 1, :]
    flab[0] = lax.select(core == 0, lab_in0, lab_entry0)
    for n in range(1, N):
        flab[n] = segc[n * BLOCK - 1 : n * BLOCK, :]
        rlab[n - 1] = segc[n * BLOCK : n * BLOCK + 1, :]

    def decayed(n, c):
        linked = segc[rows(n), :] == flab[n]
        for h in range(H):
            qd = jnp.where(linked, qv[rows(n), col(h)].astype(F32) * wf[h], 0.0)
            qc[rows(n), col(h)] = qd.astype(BF16)
        return c

    lax.fori_loop(N // 2, N, intra, 0)
    lax.fori_loop(0, N, decayed, 0)

    def chain(h, incoming):
        lam = pows[0, h]
        pb = pows[1, h]
        state = lam * incoming
        for n in range(N):
            sst[n, h] = state.astype(BF16)
            if n < N - 1:
                keep = flab[n] == flab[n + 1]
                state = jnp.where(keep, pb, 0.0) * state + lam * fst[n, h]

    row16 = lax.broadcasted_iota(jnp.int32, (16, HD), 0)

    def cross(n, h0):
        sq = jnp.zeros((BLOCK, HD), F32)
        da = jnp.zeros((BLOCK, HD), F32)
        for i in range(HH):
            h = h0 + i
            a = attn[rows(n), col(h)] + nn(qc[rows(n), col(h)], sst[n, h])
            attn[rows(n), col(h)] = a
            sq = sq + a * a
            da = da + dzs[rows(n), col(h)] * a
        return sq, da

    def cross_own(n, c):
        sq, da = cross(n, own0)
        ssq[rows(n), :] = sq
        sda[rows(n), :] = da
        return c

    def cross_other(n, total):
        sq, da = cross(n, other0)
        pick1 = jnp.where(row16 == n, 1.0, 0.0).astype(BF16)
        pick2 = jnp.where(row16 == n + N, 1.0, 0.0).astype(BF16)
        sq = (sq + ssq[rows(n), :]).astype(BF16)
        da = (da + sda[rows(n), :]).astype(BF16)
        return total + nt(pick1, sq) + nt(pick2, da)

    drain(ebuf0, CX - 1, rsem.at[2])
    kept = hand_over(0, fen, ebuf0, lab_entry0, lab_in0, qbs0)
    post0 = remote(qbs0, qbr0, 3, mate, zme)
    post0.start()
    for i in range(HH):
        chain(own0 + i, kept[i])
    lax.fori_loop(0, N, cross_own, 0)
    post0.wait_recv()
    for i in range(HH):
        chain(other0 + i, qbr0[i * HD : (i + 1) * HD, :])
    total = lax.fori_loop(0, N, cross_other, jnp.zeros((16, BLOCK), F32))
    zbuf[zme] = total[0 : 2 * N, :]

    zorder = sorted(range(1, Z), key=lambda i: min(i, Z - i), reverse=True)
    for i in zorder:
        remote(zbuf.at[zme], zbuf.at[zme], 4, me, lax.rem(zme + i, Z)).start()

    def turn(n, c):
        first = segc[pl.ds(n * BLOCK, 1), :]
        here = segc[rows(n), :] == first
        for h in range(H):
            qw = jnp.where(here, qv[rows(n), col(h)].astype(F32) * wf[h], 0.0)
            qwt[n, h] = qw.T.astype(BF16)
        return c

    lax.fori_loop(0, N, turn, 0)

    feats = float(H * HD * Z)
    wide = 2 * N * HD
    rr = lax.broadcasted_iota(jnp.int32, (4 * N, wide), 0)
    cc = lax.broadcasted_iota(jnp.int32, (4 * N, wide), 1) // HD
    picks = jnp.where((rr == cc) | (rr == cc + 2 * N), 1.0, 0.0).astype(BF16)
    drain(zbuf, Z - 1, rsem.at[4])
    tot = zbuf[0]
    for i in range(1, Z):
        tot = tot + zbuf[i]
    rat = lax.rsqrt(tot[0:N] / feats + EPS)
    cor = rat * rat * rat * (tot[N : 2 * N] / feats)
    both = jnp.concatenate([rat, cor], axis=0)
    upper = both.astype(BF16).astype(F32)
    lhs = jnp.concatenate([upper, both - upper], axis=0).astype(BF16)
    bc[...] = tn(lhs, picks)

    def factor(n):
        if isinstance(n, int):
            return bc[:, n * HD : (n + 1) * HD]
        return bc[:, pl.ds(pl.multiple_of(n * HD, HD), HD)]

    def reverse_state(h):
        own = None
        pb = pows[1, h]
        for n in reversed(range(N)):
            d = (factor(n) * dzs[rows(n), col(h)] - factor(N + n) * attn[rows(n), col(h)]).astype(BF16)
            datt[rows(n), col(h)] = d
            f = nn(qwt[n, h], d)
            rst[n, h] = f
            if own is None:
                own = f
            else:
                first = segc[n * BLOCK : n * BLOCK + 1, :]
                after = segc[(n + 1) * BLOCK : (n + 1) * BLOCK + 1, :]
                own = jnp.where(first == after, pb, 0.0) * own + f
        return own

    for i in range(HH):
        pbs1[i * HD : (i + 1) * HD, :] = reverse_state(other0 + i)
    pair1 = remote(pbs1, pbr1, 5, mate, zme)
    pair1.start()
    for i in range(HH):
        hfs[i * HD : (i + 1) * HD, :] = reverse_state(own0 + i)
    pair1.wait_recv()
    lab_entry1, lab_exit1 = merge(1, pbr1, myfirst, matefirst, fen1, fbuf1)
    for x in range(CX):
        fbuf1[x, SR : SR + 1, :] = lab_exit1
    scatter(fbuf1, rbuf1, 6, CY - 1, 0, CX)

    def gated(n, sums):
        out = []
        for h in range(H):
            normed = attn[rows(n), col(h)] * factor(n)
            sig = jax.nn.sigmoid(gv[rows(n), col(h)].astype(F32))
            t = ov[rows(n), col(h)].astype(F32) * sig * normed
            ggv[rows(n), col(h)] = (t * gain_ref[0:1, col(h)] * (1.0 - sig)).astype(BF16)
            out.append(sums[h] + jnp.sum(t.reshape(BLOCK // 8, 8, HD), axis=0))
        return tuple(out)

    sums = lax.fori_loop(0, N, gated, tuple(jnp.zeros((8, HD), F32) for _ in range(H)))
    gbuf[mcol] = jnp.concatenate([jnp.sum(s, axis=0, keepdims=True) for s in sums], axis=1)

    def gain_row(i, c):
        remote(gbuf.at[mcol], gbuf.at[mcol], 7, row0 + lax.rem(mcol + i, RW), zme).start()
        return c

    lax.fori_loop(1, RW, gain_row, 0)

    def back(n, c):
        same = same_of(n)
        linked = segc[rows(n), :] == flab[n]
        for h in range(H):
            d = datt[rows(n), col(h)]
            s = nt(d, vv[rows(n), col(h)])
            ds = jnp.where(same, s * wb[h], 0.0).astype(BF16)
            dq = nn(ds, kv[rows(n), col(h)])
            dq = dq + jnp.where(linked, wf[h], 0.0) * nt(d, sst[n, h])
            dqv[rows(n), col(h)] = dq.astype(BF16)
            dkp[rows(n), col(h)] = tn(ds, qv[rows(n), col(h)])
            dvp[rows(n), col(h)] = tn(sw[n, h], d)
        return c

    lax.fori_loop(0, N // 2, back, 0)

    drain(rbuf1, 2 * CX - 1, rsem.at[6])
    acc = rbuf1[2 * CX - 1, 0:SR, :]
    for i in reversed(range(2 * CX - 1)):
        if i < CX:
            sbuf1[i] = acc
        if i > 0:
            linked = rbuf1[i + 1, SR : SR + 1, :] == rbuf1[i, SR : SR + 1, :]
            acc = rbuf1[i, 0:SR, :] + jnp.where(linked, pchip, 0.0) * acc
    spread(sbuf1, ebuf1, 8)

    drain(gbuf, RW - 1, rsem.at[7])
    part = gbuf[0]
    for i in range(1, RW):
        part = part + gbuf[i]
    cbuf[mrow] = part

    def gain_col(i, c):
        other = lax.rem(mrow + i, CW)
        remote(cbuf.at[mrow], cbuf.at[mrow], 9, other * RW + mcol, zme).start()
        return c

    lax.fori_loop(1, CW, gain_col, 0)

    lax.fori_loop(N // 2, N, back, 0)

    drain(cbuf, CW - 1, rsem.at[9])
    part = cbuf[0]
    for i in range(1, CW):
        part = part + cbuf[i]
    dgain_ref[...] = part

    def finish(h, incoming):
        lam = pows[0, h]
        pb = pows[1, h]
        state = lam * incoming
        for n in reversed(range(N)):
            rin = state.astype(BF16)
            w = jnp.where(segc[rows(n), :] == rlab[n], wl[h], 0.0)
            dk = dkp[rows(n), col(h)] + w * nt(vv[rows(n), col(h)], rin)
            dv = dvp[rows(n), col(h)] + w * nn(kv[rows(n), col(h)], rin)
            dkv[rows(n), col(h)] = dk.astype(BF16)
            dvv[rows(n), col(h)] = dv.astype(BF16)
            if n > 0:
                keep = rlab[n] == rlab[n - 1]
                state = jnp.where(keep, pb, 0.0) * state + lam * rst[n, h]

    lab_in1 = rbuf1[chipx + 1, SR : SR + 1, :]
    drain(ebuf1, CX - 1, rsem.at[8])
    kept = hand_over(1, fen1, ebuf1, lab_entry1, lab_in1, qbs1)
    rlab[N - 1] = lax.select(core == 1, lab_in1, lab_entry1)
    post1 = remote(qbs1, qbr1, 10, mate, zme)
    post1.start()
    for i in range(HH):
        finish(own0 + i, kept[i])
    post1.wait_recv()
    for i in range(HH):
        finish(other0 + i, qbr1[i * HD : (i + 1) * HD, :])
    for copy in (pair0, post0, pair1, post1):
        copy.wait_send()
    drain(rbuf0, 2 * CX - 1, ssem.at[1])
    drain(sbuf0, CX - 1, ssem.at[2])
    drain(zbuf, Z - 1, ssem.at[4])
    drain(rbuf1, 2 * CX - 1, ssem.at[6])
    drain(gbuf, RW - 1, ssem.at[7])
    drain(sbuf1, CX - 1, ssem.at[8])
    drain(cbuf, CW - 1, ssem.at[9])


def mover(*refs):
    half = len(refs) // 2
    sems = refs[-1]
    copies = [
        pltpu.make_async_copy(refs[i], refs[half + i], sems.at[i]) for i in range(half)
    ]
    for copy in copies:
        copy.start()
    for copy in copies:
        copy.wait()


def body(queries, keys, values, gate, grad_out, gain, decay_rate, segment_ids):
    R = lax.axis_size("ctx")
    Z = lax.axis_size("head")
    T, W = queries.shape
    H = W // HD
    N = T // BLOCK
    RW = 8 if R == 32 else R // 2
    CW = R // RW
    CX = 4
    HR = H * HD // 2
    SR = HR // CX
    hbm = pl.BlockSpec(memory_space=pltpu.HBM)
    vspec = pl.BlockSpec(memory_space=pltpu.VMEM)
    big = jax.ShapeDtypeStruct((T, W), BF16)
    small = jax.ShapeDtypeStruct((1, W), F32)
    VM = pltpu.VMEM
    scratch = (
        [VM((T, W), BF16)] * 5
        + [VM((1, W), F32), pltpu.SMEM((H,), F32), VM((1, T), jnp.int32)]
        + [
            VM((T, HD), F32),
            VM((H, BLOCK, HD), F32),
            VM((H, BLOCK, HD), F32),
            VM((H, BLOCK, BLOCK), F32),
            VM((N, H, HD, HD), F32),
            VM((N, H, BLOCK, BLOCK), BF16),
            VM((T, W), F32),
            VM((T, W), F32),
            VM((N, H, HD, HD), BF16),
            VM((BLOCK, 2 * N * HD), F32),
            VM((N, H, HD, BLOCK), BF16),
            VM((T, W), BF16),
            VM((N, H, HD, HD), F32),
            VM((T, W), F32),
            VM((T, W), F32),
            VM((T, HD), F32),
            VM((T, HD), F32),
            VM((T, W), BF16),
            VM((4, H, 1, HD), F32),
        ]
        + [VM((HR + 8, HD), F32)] * 2
        + [VM((HR, HD), F32)] * 2
        + [VM((CX, SR + 8, HD), F32), VM((2 * CX, SR + 8, HD), F32)]
        + [VM((CX, SR, HD), F32)] * 2
        + [VM((HR, HD), F32)] * 2
        + [VM((HR + 8, HD), F32)] * 2
        + [VM((HR, HD), F32)]
        + [VM((CX, SR + 8, HD), F32), VM((2 * CX, SR + 8, HD), F32)]
        + [VM((CX, SR, HD), F32)] * 2
        + [VM((HR, HD), F32)] * 2
        + [
            VM((N, 1, HD), F32),
            VM((N, 1, HD), F32),
            VM((Z, 2 * N, BLOCK), F32),
            VM((RW, 1, W), F32),
            VM((CW, 1, W), F32),
            pltpu.SemaphoreType.DMA((8,)),
            pltpu.SemaphoreType.DMA((11,)),
            pltpu.SemaphoreType.DMA((11,)),
        ]
    )
    outs = pl.pallas_call(
        functools.partial(kernel, (R, Z, RW, N, H)),
        out_shape=(big, big, big, big, small),
        in_specs=[hbm] * 8,
        out_specs=(vspec,) * 5,
        scratch_shapes=scratch,
        compiler_params=pltpu.CompilerParams(
            collective_id=0, has_side_effects=True, vmem_limit_bytes=VMEM_A
        ),
    )(
        queries, keys, values, gate, grad_out,
        gain.reshape(1, W), decay_rate, segment_ids.reshape(1, T),
    )
    moved = pl.pallas_call(
        mover,
        out_shape=(big, big, big, big, small),
        in_specs=[vspec] * 5,
        out_specs=(hbm,) * 5,
        scratch_shapes=[pltpu.SemaphoreType.DMA((5,))],
        compiler_params=pltpu.CompilerParams(vmem_limit_bytes=VMEM_B),
    )(*outs)
    dq, dk, dv, gg, dgain = moved
    return dq, dk, dv, gg, dgain.reshape(W)


def solution(mesh):
    in_specs = (P("ctx", "head"),) * 5 + (P("head"), P("head"), P("ctx"))
    out_specs = (P("ctx", "head"),) * 4 + (P("head"),)
    return jax.shard_map(body, mesh=mesh, in_specs=in_specs, out_specs=out_specs, check_vma=False)
```

```python
import functools

import jax
import jax.numpy as jnp
from jax import lax
from jax.experimental import pallas as pl
from jax.experimental.pallas import tpu as pltpu
from jax.sharding import PartitionSpec as P

MESH = pl.DeviceIdType.MESH
F32 = jnp.float32
BF16 = jnp.bfloat16
BLOCK = 256
HD = 128
EPS = 1e-06
VMEM_A = 49 * 1024 * 1024
VMEM_B = 8 * 1024 * 1024


def nn(a, b):
    return lax.dot_general(a, b, (((1,), (0,)), ((), ())), preferred_element_type=F32)


def nt(a, b):
    return lax.dot_general(a, b, (((1,), (1,)), ((), ())), preferred_element_type=F32)


def tn(a, b):
    return lax.dot_general(a, b, (((0,), (0,)), ((), ())), preferred_element_type=F32)


def drain(ref, count, sem):
    if count == 0:
        return
    part = ref.at[pl.ds(0, count)]
    pltpu.make_async_copy(part, part, sem).wait()


def kernel(
    dims,
    q_hbm, k_hbm, v_hbm, g_hbm, o_hbm, small_hbm, seg_hbm,
    dqv, dkv, dvv, ggv, dgain_ref,
    qv, kv, vv, gv, ov, small_ref, seg_ref,
    segc, wl, wf, wb, fst, sw, attn, dzs, sst, bc, qwt, datt, rst, dkp, dvp, ssq, sda, qc, pows,
    pbs0, pbr0, hfs, fen, fbuf0, rbuf0, sbuf0, ebuf0, qbs0, qbr0,
    pbs1, pbr1, fen1, fbuf1, rbuf1, sbuf1, ebuf1, qbs1, qbr1,
    flab, rlab, zbuf, gps, gpr, gbuf, cbuf,
    in_sem, ssem, rsem,
):
    R, Z, N, H = dims
    T = N * BLOCK
    C = R // 2
    HH = H // 2
    HR = HH * HD
    CX = 4
    SR = HR // CX
    HJ = CX // HH
    CY = C // CX
    me = lax.axis_index("ctx")
    zme = lax.axis_index("head")
    core = lax.rem(me, 2)
    mate = me + 1 - 2 * core
    chip = me // 2
    chipy = chip // CX
    chipx = lax.rem(chip, CX)
    own0 = HH * core
    other0 = HH * (1 - core)

    loads = [
        pltpu.make_async_copy(src, dst, in_sem.at[i])
        for i, (src, dst) in enumerate(
            (
                (seg_hbm, seg_ref), (small_hbm, small_ref), (k_hbm, kv), (v_hbm, vv),
                (q_hbm, qv), (g_hbm, gv), (o_hbm, ov),
            )
        )
    ]
    for copy in loads[:4]:
        copy.start()

    barrier = pltpu.get_barrier_semaphore()

    def greet(ctx, head):
        pl.semaphore_signal(barrier, inc=1, device_id=(ctx, head), device_id_type=MESH)

    heads = sorted(range(1, Z), key=lambda i: min(i, Z - i), reverse=True)
    near = {(dy, dx) for dy in (0, 1, CY - 1) for dx in range(CX)}
    near = sorted((near | {(dy, 0) for dy in range(CY)}) - {(0, 0)}, reverse=True)
    for i in heads:
        greet(me, lax.rem(zme + i, Z))
    for dy, dx in near:
        y, x = lax.rem(chipy + dy, CY), lax.rem(chipx + dx, CX)
        greet(2 * (y * CX + x) + core, zme)
    greet(mate, zme)
    greeted = len(heads) + len(near) + 1
    for copy in loads[4:]:
        copy.start()

    def remote(src, dst, phase, ctx, head):
        return pltpu.make_async_remote_copy(
            src_ref=src, dst_ref=dst, send_sem=ssem.at[phase], recv_sem=rsem.at[phase],
            device_id=(ctx, head), device_id_type=MESH,
        )

    def col(h):
        start = h * HD
        return pl.ds(start if isinstance(h, int) else pl.multiple_of(start, HD), HD)

    def rows(n):
        start = n * BLOCK
        return pl.ds(start if isinstance(n, int) else pl.multiple_of(start, BLOCK), BLOCK)

    def rate(h):
        return small_ref[H + h : H + h + 1, :]

    def gain(h):
        return small_ref[h : h + 1, :]

    def power(h, times):
        return jnp.exp(rate(h) * -times)

    iota = lax.broadcasted_iota(jnp.int32, (BLOCK, HD), 0).astype(F32)
    first_row = jnp.where(lax.broadcasted_iota(jnp.int32, (16, HD), 0) == 0, 1.0, 0.0).astype(BF16)
    loads[0].wait()
    for n in range(N):
        seg = jnp.broadcast_to(seg_ref[0:1, rows(n)].astype(F32), (16, BLOCK)).astype(BF16)
        segc[rows(n), :] = tn(seg, first_row)
    loads[1].wait()
    for h in range(H):
        wl[h] = jnp.exp(-rate(h) * (BLOCK - 1.0 - iota))
        for i, times in enumerate((1.0, float(BLOCK), float(T), 2.0 * T)):
            pows[i, h] = power(h, times)
    mylast = segc[T - 1 : T, :]
    myfirst = segc[0:1, :]

    def at_chip(y, x):
        return 2 * (y * CX + x) + core

    around = (2, 1, 3)

    def merge(entry, pbr, lab_m, lab_p, fen_ref, fbuf):
        is_entry = core == entry
        lab_entry = lax.select(is_entry, lab_m, lab_p)
        lab_exit = lax.select(is_entry, lab_p, lab_m)
        for i in range(HH):
            part = slice(i * HD, (i + 1) * HD)
            fm = hfs[part, :]
            fp = pbr[part, :]
            fe = lax.select(is_entry, fm, fp)
            fx = lax.select(is_entry, fp, fm)
            fen_ref[part, :] = fe
            c = fx + jnp.where(lab_entry == lab_exit, pows[2, own0 + i], 0.0) * fe
            fbuf[i * HJ : (i + 1) * HJ, 0:SR, :] = c.reshape(HJ, SR, HD)
        return lab_entry, lab_exit

    def hand_over(entry, fen_ref, ebuf, lab_entry, lab_in, qbs):
        is_entry = core == entry
        kept = []
        for i in range(HH):
            part = slice(i * HD, (i + 1) * HD)
            ve = ebuf[i * HJ : (i + 1) * HJ].reshape(HD, HD)
            linked = jnp.where(lab_in == lab_entry, pows[2, own0 + i], 0.0)
            vx = fen_ref[part, :] + linked * ve
            qbs[part, :] = lax.select(is_entry, vx, ve)
            kept.append(lax.select(is_entry, ve, vx))
        return kept

    def device_state(h):
        own = None
        pb = pows[1, h]
        w = wl[h]
        for n in range(N):
            last = segc[n * BLOCK + BLOCK - 1 : n * BLOCK + BLOCK, :]
            here = segc[rows(n), :] == last
            kw = jnp.where(here, kv[rows(n), col(h)].astype(F32) * w, 0.0).astype(BF16)
            f = tn(kw, vv[rows(n), col(h)])
            fst[n, h] = f
            if own is None:
                own = f
            else:
                before = segc[n * BLOCK - 1 : n * BLOCK, :]
                own = jnp.where(before == last, pb, 0.0) * own + f
        return own

    loads[2].wait()
    loads[3].wait()
    for i in range(HH):
        pbs0[i * HD : (i + 1) * HD, :] = device_state(other0 + i)
    top = lax.broadcasted_iota(jnp.int32, (8, HD), 0) == 0
    pbs0[HR : HR + 8, :] = jnp.where(top, mylast, myfirst)
    pl.semaphore_wait(barrier, greeted)
    pair0 = remote(pbs0, pbr0, 0, mate, zme)
    pair0.start()
    for i in range(HH):
        hfs[i * HD : (i + 1) * HD, :] = device_state(own0 + i)
    pair0.wait_recv()
    matelast = pbr0[HR : HR + 1, :]
    matefirst = pbr0[HR + 1 : HR + 2, :]
    lab_entry0, lab_exit0 = merge(0, pbr0, mylast, matelast, fen, fbuf0)
    for x in range(CX):
        fbuf0[x, SR : SR + 1, :] = lab_exit0

    def scatter(fbuf, rbuf, phase, turn_y, near, far):
        there = lax.rem(chipy + turn_y, CY)
        for dx in (2, 1, 3, 0):
            x = lax.rem(chipx + dx, CX)
            remote(fbuf.at[x], rbuf.at[far + chipx], phase, at_chip(there, x), zme).start()
        for dx in around:
            x = lax.rem(chipx + dx, CX)
            remote(fbuf.at[x], rbuf.at[near + chipx], phase, at_chip(chipy, x), zme).start()
        rbuf[near + chipx] = fbuf[chipx]

    def spread(sbuf, ebuf, phase):
        for dx in around:
            x = lax.rem(chipx + dx, CX)
            remote(sbuf.at[x], ebuf.at[chipx], phase, at_chip(chipy, x), zme).start()
        ebuf[chipx] = sbuf[chipx]

    scatter(fbuf0, rbuf0, 1, 1, CX, 0)

    d2 = (
        lax.broadcasted_iota(jnp.int32, (BLOCK, BLOCK), 0)
        - lax.broadcasted_iota(jnp.int32, (BLOCK, BLOCK), 1)
    ).astype(F32)
    for h in range(H):
        wf[h] = jnp.exp(-rate(h) * iota)
        rate2 = jnp.concatenate([rate(h), rate(h)], axis=1)
        wb[h] = jnp.where(d2 >= 0, jnp.exp(-rate2 * jnp.maximum(d2, 0.0)), 0.0)

    def same_of(n):
        sc = segc[rows(n), :]
        return jnp.concatenate([sc, sc], axis=1) == seg_ref[0:1, rows(n)].astype(F32)

    def intra(n, c):
        same = same_of(n)
        for h in range(H):
            s = nt(qv[rows(n), col(h)], kv[rows(n), col(h)])
            s = jnp.where(same, s * wb[h], 0.0).astype(BF16)
            sw[n, h] = s
            attn[rows(n), col(h)] = nn(s, vv[rows(n), col(h)])
            sig = jax.nn.sigmoid(gv[rows(n), col(h)].astype(F32))
            dzs[rows(n), col(h)] = ov[rows(n), col(h)].astype(F32) * sig * gain(h)
        return c

    for copy in loads[4:]:
        copy.wait()
    lax.fori_loop(0, N // 2, intra, 0)

    pchip = pows[3, own0 + chipx // HJ]
    drain(rbuf0, 2 * CX - 1, rsem.at[1])
    acc = rbuf0[0, 0:SR, :]
    for i in range(1, 2 * CX):
        if i >= CX:
            sbuf0[i - CX] = acc
        if i < 2 * CX - 1:
            linked = rbuf0[i - 1, SR : SR + 1, :] == rbuf0[i, SR : SR + 1, :]
            acc = rbuf0[i, 0:SR, :] + jnp.where(linked, pchip, 0.0) * acc
    spread(sbuf0, ebuf0, 2)

    lab_in0 = rbuf0[CX - 1 + chipx, SR : SR + 1, :]
    flab[0] = lax.select(core == 0, lab_in0, lab_entry0)
    for n in range(1, N):
        flab[n] = segc[n * BLOCK - 1 : n * BLOCK, :]
        rlab[n - 1] = segc[n * BLOCK : n * BLOCK + 1, :]

    def decayed(n, c):
        linked = segc[rows(n), :] == flab[n]
        for h in range(H):
            qd = jnp.where(linked, qv[rows(n), col(h)].astype(F32) * wf[h], 0.0)
            qc[rows(n), col(h)] = qd.astype(BF16)
        return c

    lax.fori_loop(N // 2, N, intra, 0)
    lax.fori_loop(0, N, decayed, 0)

    def chain(h, incoming):
        lam = pows[0, h]
        pb = pows[1, h]
        state = lam * incoming
        for n in range(N):
            sst[n, h] = state.astype(BF16)
            if n < N - 1:
                keep = flab[n] == flab[n + 1]
                state = jnp.where(keep, pb, 0.0) * state + lam * fst[n, h]

    row16 = lax.broadcasted_iota(jnp.int32, (16, HD), 0)

    def cross(n, h0):
        sq = jnp.zeros((BLOCK, HD), F32)
        da = jnp.zeros((BLOCK, HD), F32)
        for i in range(HH):
            h = h0 + i
            a = attn[rows(n), col(h)] + nn(qc[rows(n), col(h)], sst[n, h])
            attn[rows(n), col(h)] = a
            sq = sq + a * a
            da = da + dzs[rows(n), col(h)] * a
        return sq, da

    def cross_own(n, c):
        sq, da = cross(n, own0)
        ssq[rows(n), :] = sq
        sda[rows(n), :] = da
        return c

    def cross_other(n, total):
        sq, da = cross(n, other0)
        pick1 = jnp.where(row16 == n, 1.0, 0.0).astype(BF16)
        pick2 = jnp.where(row16 == n + N, 1.0, 0.0).astype(BF16)
        sq = (sq + ssq[rows(n), :]).astype(BF16)
        da = (da + sda[rows(n), :]).astype(BF16)
        return total + nt(pick1, sq) + nt(pick2, da)

    drain(ebuf0, CX - 1, rsem.at[2])
    kept = hand_over(0, fen, ebuf0, lab_entry0, lab_in0, qbs0)
    post0 = remote(qbs0, qbr0, 3, mate, zme)
    post0.start()
    for i in range(HH):
        chain(own0 + i, kept[i])
    lax.fori_loop(0, N, cross_own, 0)
    post0.wait_recv()
    for i in range(HH):
        chain(other0 + i, qbr0[i * HD : (i + 1) * HD, :])
    total = lax.fori_loop(0, N, cross_other, jnp.zeros((16, BLOCK), F32))
    zbuf[zme] = total[0 : 2 * N, :]

    for i in heads:
        remote(zbuf.at[zme], zbuf.at[zme], 4, me, lax.rem(zme + i, Z)).start()

    def turn(n, c):
        first = segc[pl.ds(n * BLOCK, 1), :]
        here = segc[rows(n), :] == first
        for h in range(H):
            qw = jnp.where(here, qv[rows(n), col(h)].astype(F32) * wf[h], 0.0)
            qwt[n, h] = qw.T.astype(BF16)
        return c

    lax.fori_loop(0, N, turn, 0)

    feats = float(H * HD * Z)
    wide = 2 * N * HD
    rr = lax.broadcasted_iota(jnp.int32, (4 * N, wide), 0)
    cc = lax.broadcasted_iota(jnp.int32, (4 * N, wide), 1) // HD
    picks = jnp.where((rr == cc) | (rr == cc + 2 * N), 1.0, 0.0).astype(BF16)
    drain(zbuf, Z - 1, rsem.at[4])
    tot = zbuf[0]
    for i in range(1, Z):
        tot = tot + zbuf[i]
    rat = lax.rsqrt(tot[0:N] / feats + EPS)
    cor = rat * rat * rat * (tot[N : 2 * N] / feats)
    both = jnp.concatenate([rat, cor], axis=0)
    upper = both.astype(BF16).astype(F32)
    lhs = jnp.concatenate([upper, both - upper], axis=0).astype(BF16)
    bc[...] = tn(lhs, picks)

    def factor(n):
        if isinstance(n, int):
            return bc[:, n * HD : (n + 1) * HD]
        return bc[:, pl.ds(pl.multiple_of(n * HD, HD), HD)]

    def reverse_state(h):
        own = None
        pb = pows[1, h]
        for n in reversed(range(N)):
            d = (factor(n) * dzs[rows(n), col(h)] - factor(N + n) * attn[rows(n), col(h)]).astype(BF16)
            datt[rows(n), col(h)] = d
            f = nn(qwt[n, h], d)
            rst[n, h] = f
            if own is None:
                own = f
            else:
                first = segc[n * BLOCK : n * BLOCK + 1, :]
                after = segc[(n + 1) * BLOCK : (n + 1) * BLOCK + 1, :]
                own = jnp.where(first == after, pb, 0.0) * own + f
        return own

    for i in range(HH):
        pbs1[i * HD : (i + 1) * HD, :] = reverse_state(other0 + i)
    pair1 = remote(pbs1, pbr1, 5, mate, zme)
    pair1.start()
    for i in range(HH):
        hfs[i * HD : (i + 1) * HD, :] = reverse_state(own0 + i)
    pair1.wait_recv()
    lab_entry1, lab_exit1 = merge(1, pbr1, myfirst, matefirst, fen1, fbuf1)
    for x in range(CX):
        fbuf1[x, SR : SR + 1, :] = lab_exit1
    scatter(fbuf1, rbuf1, 6, CY - 1, 0, CX)

    def gated(n, sums):
        out = []
        for h in range(H):
            normed = attn[rows(n), col(h)] * factor(n)
            sig = jax.nn.sigmoid(gv[rows(n), col(h)].astype(F32))
            t = ov[rows(n), col(h)].astype(F32) * sig * normed
            ggv[rows(n), col(h)] = (t * gain(h) * (1.0 - sig)).astype(BF16)
            out.append(sums[h] + jnp.sum(t.reshape(BLOCK // 8, 8, HD), axis=0))
        return tuple(out)

    sums = lax.fori_loop(0, N, gated, tuple(jnp.zeros((8, HD), F32) for _ in range(H)))
    gps[...] = jnp.concatenate([jnp.sum(s, axis=0, keepdims=True) for s in sums], axis=1)
    gain_pair = remote(gps, gpr, 11, mate, zme)
    gain_pair.start()

    def back(n, c):
        same = same_of(n)
        linked = segc[rows(n), :] == flab[n]
        for h in range(H):
            d = datt[rows(n), col(h)]
            s = nt(d, vv[rows(n), col(h)])
            ds = jnp.where(same, s * wb[h], 0.0).astype(BF16)
            dq = nn(ds, kv[rows(n), col(h)])
            dq = dq + jnp.where(linked, wf[h], 0.0) * nt(d, sst[n, h])
            dqv[rows(n), col(h)] = dq.astype(BF16)
            dkp[rows(n), col(h)] = tn(ds, qv[rows(n), col(h)])
            dvp[rows(n), col(h)] = tn(sw[n, h], d)
        return c

    lax.fori_loop(0, 1, back, 0)
    gain_pair.wait_recv()
    gbuf[chipx] = gps[...] + gpr[...]
    for dx in around:
        x = lax.rem(chipx + dx, CX)
        remote(gbuf.at[chipx], gbuf.at[chipx], 7, at_chip(chipy, x), zme).start()
    lax.fori_loop(1, N // 2, back, 0)

    drain(rbuf1, 2 * CX - 1, rsem.at[6])
    acc = rbuf1[2 * CX - 1, 0:SR, :]
    for i in reversed(range(2 * CX - 1)):
        if i < CX:
            sbuf1[i] = acc
        if i > 0:
            linked = rbuf1[i + 1, SR : SR + 1, :] == rbuf1[i, SR : SR + 1, :]
            acc = rbuf1[i, 0:SR, :] + jnp.where(linked, pchip, 0.0) * acc
    spread(sbuf1, ebuf1, 8)

    drain(gbuf, CX - 1, rsem.at[7])
    part = gbuf[0]
    for i in range(1, CX):
        part = part + gbuf[i]
    cbuf[chipy] = part
    for dy in range(1, CY):
        y = lax.rem(chipy + dy, CY)
        remote(cbuf.at[chipy], cbuf.at[chipy], 9, at_chip(y, chipx), zme).start()

    lax.fori_loop(N // 2, N, back, 0)

    drain(cbuf, CY - 1, rsem.at[9])
    part = cbuf[0]
    for i in range(1, CY):
        part = part + cbuf[i]
    dgain_ref[...] = part

    def finish(h, incoming):
        lam = pows[0, h]
        pb = pows[1, h]
        state = lam * incoming
        for n in reversed(range(N)):
            rin = state.astype(BF16)
            w = jnp.where(segc[rows(n), :] == rlab[n], wl[h], 0.0)
            dk = dkp[rows(n), col(h)] + w * nt(vv[rows(n), col(h)], rin)
            dv = dvp[rows(n), col(h)] + w * nn(kv[rows(n), col(h)], rin)
            dkv[rows(n), col(h)] = dk.astype(BF16)
            dvv[rows(n), col(h)] = dv.astype(BF16)
            if n > 0:
                keep = rlab[n] == rlab[n - 1]
                state = jnp.where(keep, pb, 0.0) * state + lam * rst[n, h]

    lab_in1 = rbuf1[chipx + 1, SR : SR + 1, :]
    drain(ebuf1, CX - 1, rsem.at[8])
    kept = hand_over(1, fen1, ebuf1, lab_entry1, lab_in1, qbs1)
    rlab[N - 1] = lax.select(core == 1, lab_in1, lab_entry1)
    post1 = remote(qbs1, qbr1, 10, mate, zme)
    post1.start()
    for i in range(HH):
        finish(own0 + i, kept[i])
    post1.wait_recv()
    for i in range(HH):
        finish(other0 + i, qbr1[i * HD : (i + 1) * HD, :])
    for copy in (pair0, post0, pair1, post1, gain_pair):
        copy.wait_send()
    drain(rbuf0, 2 * CX - 1, ssem.at[1])
    drain(sbuf0, CX - 1, ssem.at[2])
    drain(zbuf, Z - 1, ssem.at[4])
    drain(rbuf1, 2 * CX - 1, ssem.at[6])
    drain(gbuf, CX - 1, ssem.at[7])
    drain(sbuf1, CX - 1, ssem.at[8])
    drain(cbuf, CY - 1, ssem.at[9])


def mover(pieces, *refs):
    half = len(refs) // 2
    sems = refs[-1]
    copies = []
    for i in range(half):
        src, dst = refs[i], refs[half + i]
        step = src.shape[0] // pieces[i]
        for j in range(pieces[i]):
            part = pl.ds(j * step, step)
            copies.append(pltpu.make_async_copy(src.at[part], dst.at[part], sems.at[len(copies)]))
    for copy in copies:
        copy.start()
    for copy in copies:
        copy.wait()


def body(queries, keys, values, gate, grad_out, gain, decay_rate, segment_ids):
    R = lax.axis_size("ctx")
    Z = lax.axis_size("head")
    T, W = queries.shape
    H = W // HD
    N = T // BLOCK
    CX = 4
    HR = H * HD // 2
    SR = HR // CX
    hbm = pl.BlockSpec(memory_space=pltpu.HBM)
    vspec = pl.BlockSpec(memory_space=pltpu.VMEM)
    big = jax.ShapeDtypeStruct((T, W), BF16)
    small = jax.ShapeDtypeStruct((1, W), F32)
    VM = pltpu.VMEM
    scratch = (
        [VM((T, W), BF16)] * 5
        + [VM((2 * H, HD), F32), VM((1, T), jnp.int32)]
        + [
            VM((T, HD), F32),
            VM((H, BLOCK, HD), F32),
            VM((H, BLOCK, HD), F32),
            VM((H, BLOCK, BLOCK), F32),
            VM((N, H, HD, HD), F32),
            VM((N, H, BLOCK, BLOCK), BF16),
            VM((T, W), F32),
            VM((T, W), F32),
            VM((N, H, HD, HD), BF16),
            VM((BLOCK, 2 * N * HD), F32),
            VM((N, H, HD, BLOCK), BF16),
            VM((T, W), BF16),
            VM((N, H, HD, HD), F32),
            VM((T, W), F32),
            VM((T, W), F32),
            VM((T, HD), F32),
            VM((T, HD), F32),
            VM((T, W), BF16),
            VM((4, H, 1, HD), F32),
        ]
        + [VM((HR + 8, HD), F32)] * 2
        + [VM((HR, HD), F32)] * 2
        + [VM((CX, SR + 8, HD), F32), VM((2 * CX, SR + 8, HD), F32)]
        + [VM((CX, SR, HD), F32)] * 2
        + [VM((HR, HD), F32)] * 2
        + [VM((HR + 8, HD), F32)] * 2
        + [VM((HR, HD), F32)]
        + [VM((CX, SR + 8, HD), F32), VM((2 * CX, SR + 8, HD), F32)]
        + [VM((CX, SR, HD), F32)] * 2
        + [VM((HR, HD), F32)] * 2
        + [
            VM((N, 1, HD), F32),
            VM((N, 1, HD), F32),
            VM((Z, 2 * N, BLOCK), F32),
            VM((1, W), F32),
            VM((1, W), F32),
            VM((CX, 1, W), F32),
            VM((R // (2 * CX), 1, W), F32),
            pltpu.SemaphoreType.DMA((7,)),
            pltpu.SemaphoreType.DMA((12,)),
            pltpu.SemaphoreType.DMA((12,)),
        ]
    )
    rates = jnp.broadcast_to(decay_rate[:, None], (H, HD))
    small_in = jnp.concatenate([gain.reshape(H, HD), rates], axis=0)
    outs = pl.pallas_call(
        functools.partial(kernel, (R, Z, N, H)),
        out_shape=(big, big, big, big, small),
        in_specs=[hbm] * 7,
        out_specs=(vspec,) * 5,
        scratch_shapes=scratch,
        compiler_params=pltpu.CompilerParams(
            collective_id=0, has_side_effects=True, vmem_limit_bytes=VMEM_A
        ),
    )(
        queries, keys, values, gate, grad_out,
        small_in, segment_ids.reshape(1, T),
    )
    pieces = (4, 4, 4, 4, 1)
    moved = pl.pallas_call(
        functools.partial(mover, pieces),
        out_shape=(big, big, big, big, small),
        in_specs=[vspec] * 5,
        out_specs=(hbm,) * 5,
        scratch_shapes=[pltpu.SemaphoreType.DMA((sum(pieces),))],
        compiler_params=pltpu.CompilerParams(vmem_limit_bytes=VMEM_B),
    )(*outs)
    dq, dk, dv, gg, dgain = moved
    return dq, dk, dv, gg, dgain.reshape(W)


def solution(mesh):
    in_specs = (P("ctx", "head"),) * 5 + (P("head"), P("head"), P("ctx"))
    out_specs = (P("ctx", "head"),) * 4 + (P("head"),)
    return jax.shard_map(body, mesh=mesh, in_specs=in_specs, out_specs=out_specs, check_vma=False)
```

```python
import functools

import jax
import jax.numpy as jnp
from jax import lax
from jax.experimental import pallas as pl
from jax.experimental.pallas import tpu as pltpu
from jax.sharding import PartitionSpec as P

MESH = pl.DeviceIdType.MESH
F32 = jnp.float32
BF16 = jnp.bfloat16
BLOCK = 256
HD = 128
EPS = 1e-06
VMEM_A = 49 * 1024 * 1024
VMEM_B = 8 * 1024 * 1024


def nn(a, b):
    return lax.dot_general(a, b, (((1,), (0,)), ((), ())), preferred_element_type=F32)


def nt(a, b):
    return lax.dot_general(a, b, (((1,), (1,)), ((), ())), preferred_element_type=F32)


def tn(a, b):
    return lax.dot_general(a, b, (((0,), (0,)), ((), ())), preferred_element_type=F32)


def drain(ref, count, sem):
    if count == 0:
        return
    part = ref.at[pl.ds(0, count)]
    pltpu.make_async_copy(part, part, sem).wait()


def kernel(
    dims,
    q_hbm, k_hbm, v_hbm, g_hbm, o_hbm, small_ref, seg_ref,
    dqv, dkv, dvv, ggv, dgain_ref,
    qv, kv, vv, gv, ov,
    segc, wl, wf, wb, fst, sw, attn, dzs, sst, bc, qwt, datt, rst, dkp, dvp, ssq, sda, qc, pows,
    pbs0, pbr0, hfs, fen, fbuf0, rbuf0, sbuf0, ebuf0, qbs0, qbr0,
    pbs1, pbr1, fen1, fbuf1, rbuf1, sbuf1, ebuf1, qbs1, qbr1,
    flab, rlab, zbuf, gps, gpr, gbuf, cbuf,
    in_sem, ssem, rsem,
):
    R, Z, N, H = dims
    T = N * BLOCK
    C = R // 2
    HH = H // 2
    HR = HH * HD
    CX = 4
    SR = HR // CX
    HJ = CX // HH
    CY = C // CX
    me = lax.axis_index("ctx")
    zme = lax.axis_index("head")
    core = lax.rem(me, 2)
    mate = me + 1 - 2 * core
    chip = me // 2
    chipy = chip // CX
    chipx = lax.rem(chip, CX)
    own0 = HH * core
    other0 = HH * (1 - core)

    def half(ref, h0):
        return ref.at[:, pl.ds(pl.multiple_of(h0 * HD, HR), HR)]

    loads = [
        pltpu.make_async_copy(src, dst, in_sem.at[i])
        for i, (src, dst) in enumerate(
            (
                (half(k_hbm, other0), half(kv, other0)), (half(v_hbm, other0), half(vv, other0)),
                (half(k_hbm, own0), half(kv, own0)), (half(v_hbm, own0), half(vv, own0)),
                (q_hbm, qv), (g_hbm, gv), (o_hbm, ov),
            )
        )
    ]
    for copy in loads[:4]:
        copy.start()

    barrier = pltpu.get_barrier_semaphore()

    def greet(ctx, head):
        pl.semaphore_signal(barrier, inc=1, device_id=(ctx, head), device_id_type=MESH)

    heads = sorted(range(1, Z), key=lambda i: min(i, Z - i), reverse=True)
    near = {(dy, dx) for dy in (0, 1, CY - 1) for dx in range(CX)}
    near = sorted((near | {(dy, 0) for dy in range(CY)}) - {(0, 0)}, reverse=True)
    for i in heads:
        greet(me, lax.rem(zme + i, Z))
    for dy, dx in near:
        y, x = lax.rem(chipy + dy, CY), lax.rem(chipx + dx, CX)
        greet(2 * (y * CX + x) + core, zme)
    greet(mate, zme)
    greeted = len(heads) + len(near) + 1
    for copy in loads[4:]:
        copy.start()

    def remote(src, dst, phase, ctx, head):
        return pltpu.make_async_remote_copy(
            src_ref=src, dst_ref=dst, send_sem=ssem.at[phase], recv_sem=rsem.at[phase],
            device_id=(ctx, head), device_id_type=MESH,
        )

    def col(h):
        start = h * HD
        return pl.ds(start if isinstance(h, int) else pl.multiple_of(start, HD), HD)

    def rows(n):
        start = n * BLOCK
        return pl.ds(start if isinstance(n, int) else pl.multiple_of(start, BLOCK), BLOCK)

    def rate(h):
        return small_ref[H + h : H + h + 1, :]

    def gain(h):
        return small_ref[h : h + 1, :]

    def power(h, times):
        return jnp.exp(rate(h) * -times)

    iota = lax.broadcasted_iota(jnp.int32, (BLOCK, HD), 0).astype(F32)
    first_row = jnp.where(lax.broadcasted_iota(jnp.int32, (16, HD), 0) == 0, 1.0, 0.0).astype(BF16)
    for n in range(N):
        seg = jnp.broadcast_to(seg_ref[0:1, rows(n)].astype(F32), (16, BLOCK)).astype(BF16)
        segc[rows(n), :] = tn(seg, first_row)
    for h in range(H):
        wl[h] = jnp.exp(-rate(h) * (BLOCK - 1.0 - iota))
        for i, times in enumerate((1.0, float(BLOCK), float(T), 2.0 * T)):
            pows[i, h] = power(h, times)
    mylast = segc[T - 1 : T, :]
    myfirst = segc[0:1, :]

    def at_chip(y, x):
        return 2 * (y * CX + x) + core

    around = (2, 1, 3)

    def merge(entry, pbr, lab_m, lab_p, fen_ref, fbuf):
        is_entry = core == entry
        lab_entry = lax.select(is_entry, lab_m, lab_p)
        lab_exit = lax.select(is_entry, lab_p, lab_m)
        for i in range(HH):
            part = slice(i * HD, (i + 1) * HD)
            fm = hfs[part, :]
            fp = pbr[part, :]
            fe = lax.select(is_entry, fm, fp)
            fx = lax.select(is_entry, fp, fm)
            fen_ref[part, :] = fe
            c = fx + jnp.where(lab_entry == lab_exit, pows[2, own0 + i], 0.0) * fe
            fbuf[i * HJ : (i + 1) * HJ, 0:SR, :] = c.reshape(HJ, SR, HD)
        return lab_entry, lab_exit

    def hand_over(entry, fen_ref, ebuf, lab_entry, lab_in, qbs):
        is_entry = core == entry
        kept = []
        for i in range(HH):
            part = slice(i * HD, (i + 1) * HD)
            ve = ebuf[i * HJ : (i + 1) * HJ].reshape(HD, HD)
            linked = jnp.where(lab_in == lab_entry, pows[2, own0 + i], 0.0)
            vx = fen_ref[part, :] + linked * ve
            qbs[part, :] = lax.select(is_entry, vx, ve)
            kept.append(lax.select(is_entry, ve, vx))
        return kept

    def device_state(h):
        own = None
        pb = pows[1, h]
        w = wl[h]
        for n in range(N):
            last = segc[n * BLOCK + BLOCK - 1 : n * BLOCK + BLOCK, :]
            here = segc[rows(n), :] == last
            kw = jnp.where(here, kv[rows(n), col(h)].astype(F32) * w, 0.0).astype(BF16)
            f = tn(kw, vv[rows(n), col(h)])
            fst[n, h] = f
            if own is None:
                own = f
            else:
                before = segc[n * BLOCK - 1 : n * BLOCK, :]
                own = jnp.where(before == last, pb, 0.0) * own + f
        return own

    loads[0].wait()
    loads[1].wait()
    for i in range(HH):
        pbs0[i * HD : (i + 1) * HD, :] = device_state(other0 + i)
    top = lax.broadcasted_iota(jnp.int32, (8, HD), 0) == 0
    pbs0[HR : HR + 8, :] = jnp.where(top, mylast, myfirst)
    pl.semaphore_wait(barrier, greeted)
    pair0 = remote(pbs0, pbr0, 0, mate, zme)
    pair0.start()
    loads[2].wait()
    loads[3].wait()
    for i in range(HH):
        hfs[i * HD : (i + 1) * HD, :] = device_state(own0 + i)
    pair0.wait_recv()
    matelast = pbr0[HR : HR + 1, :]
    matefirst = pbr0[HR + 1 : HR + 2, :]
    lab_entry0, lab_exit0 = merge(0, pbr0, mylast, matelast, fen, fbuf0)
    for x in range(CX):
        fbuf0[x, SR : SR + 1, :] = lab_exit0

    def scatter(fbuf, rbuf, phase, turn_y, near, far):
        there = lax.rem(chipy + turn_y, CY)
        for dx in (2, 1, 3, 0):
            x = lax.rem(chipx + dx, CX)
            remote(fbuf.at[x], rbuf.at[far + chipx], phase, at_chip(there, x), zme).start()
        for dx in around:
            x = lax.rem(chipx + dx, CX)
            remote(fbuf.at[x], rbuf.at[near + chipx], phase, at_chip(chipy, x), zme).start()
        rbuf[near + chipx] = fbuf[chipx]

    def spread(sbuf, ebuf, phase):
        for dx in around:
            x = lax.rem(chipx + dx, CX)
            remote(sbuf.at[x], ebuf.at[chipx], phase, at_chip(chipy, x), zme).start()
        ebuf[chipx] = sbuf[chipx]

    scatter(fbuf0, rbuf0, 1, 1, CX, 0)

    d2 = (
        lax.broadcasted_iota(jnp.int32, (BLOCK, BLOCK), 0)
        - lax.broadcasted_iota(jnp.int32, (BLOCK, BLOCK), 1)
    ).astype(F32)
    for h in range(H):
        wf[h] = jnp.exp(-rate(h) * iota)
        rate2 = jnp.concatenate([rate(h), rate(h)], axis=1)
        wb[h] = jnp.where(d2 >= 0, jnp.exp(-rate2 * jnp.maximum(d2, 0.0)), 0.0)

    def same_of(n):
        sc = segc[rows(n), :]
        return jnp.concatenate([sc, sc], axis=1) == seg_ref[0:1, rows(n)].astype(F32)

    def intra(n, c):
        same = same_of(n)
        for h in range(H):
            s = nt(qv[rows(n), col(h)], kv[rows(n), col(h)])
            s = jnp.where(same, s * wb[h], 0.0).astype(BF16)
            sw[n, h] = s
            attn[rows(n), col(h)] = nn(s, vv[rows(n), col(h)])
            sig = jax.nn.sigmoid(gv[rows(n), col(h)].astype(F32))
            dzs[rows(n), col(h)] = ov[rows(n), col(h)].astype(F32) * sig * gain(h)
        return c

    for copy in loads[4:]:
        copy.wait()
    lax.fori_loop(0, N // 2, intra, 0)

    pchip = pows[3, own0 + chipx // HJ]
    drain(rbuf0, 2 * CX - 1, rsem.at[1])
    acc = rbuf0[0, 0:SR, :]
    for i in range(1, 2 * CX):
        if i >= CX:
            sbuf0[i - CX] = acc
        if i < 2 * CX - 1:
            linked = rbuf0[i - 1, SR : SR + 1, :] == rbuf0[i, SR : SR + 1, :]
            acc = rbuf0[i, 0:SR, :] + jnp.where(linked, pchip, 0.0) * acc
    spread(sbuf0, ebuf0, 2)

    lab_in0 = rbuf0[CX - 1 + chipx, SR : SR + 1, :]
    flab[0] = lax.select(core == 0, lab_in0, lab_entry0)
    for n in range(1, N):
        flab[n] = segc[n * BLOCK - 1 : n * BLOCK, :]
        rlab[n - 1] = segc[n * BLOCK : n * BLOCK + 1, :]

    def decayed(n, c):
        linked = segc[rows(n), :] == flab[n]
        for h in range(H):
            qd = jnp.where(linked, qv[rows(n), col(h)].astype(F32) * wf[h], 0.0)
            qc[rows(n), col(h)] = qd.astype(BF16)
        return c

    lax.fori_loop(N // 2, N, intra, 0)
    lax.fori_loop(0, N, decayed, 0)

    def chain(h, incoming):
        lam = pows[0, h]
        pb = pows[1, h]
        state = lam * incoming
        for n in range(N):
            sst[n, h] = state.astype(BF16)
            if n < N - 1:
                keep = flab[n] == flab[n + 1]
                state = jnp.where(keep, pb, 0.0) * state + lam * fst[n, h]

    row16 = lax.broadcasted_iota(jnp.int32, (16, HD), 0)

    def cross(n, h0):
        sq = jnp.zeros((BLOCK, HD), F32)
        da = jnp.zeros((BLOCK, HD), F32)
        for i in range(HH):
            h = h0 + i
            a = attn[rows(n), col(h)] + nn(qc[rows(n), col(h)], sst[n, h])
            attn[rows(n), col(h)] = a
            sq = sq + a * a
            da = da + dzs[rows(n), col(h)] * a
        return sq, da

    def cross_own(n, c):
        sq, da = cross(n, own0)
        ssq[rows(n), :] = sq
        sda[rows(n), :] = da
        return c

    def cross_other(n, total):
        sq, da = cross(n, other0)
        pick1 = jnp.where(row16 == n, 1.0, 0.0).astype(BF16)
        pick2 = jnp.where(row16 == n + N, 1.0, 0.0).astype(BF16)
        sq = (sq + ssq[rows(n), :]).astype(BF16)
        da = (da + sda[rows(n), :]).astype(BF16)
        return total + nt(pick1, sq) + nt(pick2, da)

    drain(ebuf0, CX - 1, rsem.at[2])
    kept = hand_over(0, fen, ebuf0, lab_entry0, lab_in0, qbs0)
    post0 = remote(qbs0, qbr0, 3, mate, zme)
    post0.start()
    for i in range(HH):
        chain(own0 + i, kept[i])
    for n in range(N):
        cross_own(n, 0)
    post0.wait_recv()
    for i in range(HH):
        chain(other0 + i, qbr0[i * HD : (i + 1) * HD, :])
    total = jnp.zeros((16, BLOCK), F32)
    for n in range(N):
        total = cross_other(n, total)
    zbuf[zme] = total[0 : 2 * N, :]

    for i in heads:
        remote(zbuf.at[zme], zbuf.at[zme], 4, me, lax.rem(zme + i, Z)).start()

    def turn(n, c):
        first = segc[pl.ds(n * BLOCK, 1), :]
        here = segc[rows(n), :] == first
        for h in range(H):
            qw = jnp.where(here, qv[rows(n), col(h)].astype(F32) * wf[h], 0.0)
            qwt[n, h] = qw.T.astype(BF16)
        return c

    lax.fori_loop(0, N, turn, 0)

    feats = float(H * HD * Z)
    wide = 2 * N * HD
    rr = lax.broadcasted_iota(jnp.int32, (4 * N, wide), 0)
    cc = lax.broadcasted_iota(jnp.int32, (4 * N, wide), 1) // HD
    picks = jnp.where((rr == cc) | (rr == cc + 2 * N), 1.0, 0.0).astype(BF16)
    drain(zbuf, Z - 1, rsem.at[4])
    tot = zbuf[0]
    for i in range(1, Z):
        tot = tot + zbuf[i]
    rat = lax.rsqrt(tot[0:N] / feats + EPS)
    cor = rat * rat * rat * (tot[N : 2 * N] / feats)
    both = jnp.concatenate([rat, cor], axis=0)
    upper = both.astype(BF16).astype(F32)
    lhs = jnp.concatenate([upper, both - upper], axis=0).astype(BF16)
    bc[...] = tn(lhs, picks)

    def factor(n):
        if isinstance(n, int):
            return bc[:, n * HD : (n + 1) * HD]
        return bc[:, pl.ds(pl.multiple_of(n * HD, HD), HD)]

    def reverse_state(h):
        own = None
        pb = pows[1, h]
        for n in reversed(range(N)):
            d = (factor(n) * dzs[rows(n), col(h)] - factor(N + n) * attn[rows(n), col(h)]).astype(BF16)
            datt[rows(n), col(h)] = d
            f = nn(qwt[n, h], d)
            rst[n, h] = f
            if own is None:
                own = f
            else:
                first = segc[n * BLOCK : n * BLOCK + 1, :]
                after = segc[(n + 1) * BLOCK : (n + 1) * BLOCK + 1, :]
                own = jnp.where(first == after, pb, 0.0) * own + f
        return own

    for i in range(HH):
        pbs1[i * HD : (i + 1) * HD, :] = reverse_state(other0 + i)
    pair1 = remote(pbs1, pbr1, 5, mate, zme)
    pair1.start()
    for i in range(HH):
        hfs[i * HD : (i + 1) * HD, :] = reverse_state(own0 + i)
    pair1.wait_recv()
    lab_entry1, lab_exit1 = merge(1, pbr1, myfirst, matefirst, fen1, fbuf1)
    for x in range(CX):
        fbuf1[x, SR : SR + 1, :] = lab_exit1
    scatter(fbuf1, rbuf1, 6, CY - 1, 0, CX)

    def gated(n, sums):
        out = []
        for h in range(H):
            normed = attn[rows(n), col(h)] * factor(n)
            sig = jax.nn.sigmoid(gv[rows(n), col(h)].astype(F32))
            t = ov[rows(n), col(h)].astype(F32) * sig * normed
            ggv[rows(n), col(h)] = (t * gain(h) * (1.0 - sig)).astype(BF16)
            out.append(sums[h] + jnp.sum(t.reshape(BLOCK // 8, 8, HD), axis=0))
        return tuple(out)

    sums = lax.fori_loop(0, N, gated, tuple(jnp.zeros((8, HD), F32) for _ in range(H)))
    gps[...] = jnp.concatenate([jnp.sum(s, axis=0, keepdims=True) for s in sums], axis=1)
    gain_pair = remote(gps, gpr, 11, mate, zme)
    gain_pair.start()

    def back(n, c):
        same = same_of(n)
        linked = segc[rows(n), :] == flab[n]
        for h in range(H):
            d = datt[rows(n), col(h)]
            s = nt(d, vv[rows(n), col(h)])
            ds = jnp.where(same, s * wb[h], 0.0).astype(BF16)
            dq = nn(ds, kv[rows(n), col(h)])
            dq = dq + jnp.where(linked, wf[h], 0.0) * nt(d, sst[n, h])
            dqv[rows(n), col(h)] = dq.astype(BF16)
            dkp[rows(n), col(h)] = tn(ds, qv[rows(n), col(h)])
            dvp[rows(n), col(h)] = tn(sw[n, h], d)
        return c

    lax.fori_loop(0, 1, back, 0)
    gain_pair.wait_recv()
    gbuf[chipx] = gps[...] + gpr[...]
    for dx in around:
        x = lax.rem(chipx + dx, CX)
        remote(gbuf.at[chipx], gbuf.at[chipx], 7, at_chip(chipy, x), zme).start()
    lax.fori_loop(1, N // 2, back, 0)

    drain(rbuf1, 2 * CX - 1, rsem.at[6])
    acc = rbuf1[2 * CX - 1, 0:SR, :]
    for i in reversed(range(2 * CX - 1)):
        if i < CX:
            sbuf1[i] = acc
        if i > 0:
            linked = rbuf1[i + 1, SR : SR + 1, :] == rbuf1[i, SR : SR + 1, :]
            acc = rbuf1[i, 0:SR, :] + jnp.where(linked, pchip, 0.0) * acc
    spread(sbuf1, ebuf1, 8)

    drain(gbuf, CX - 1, rsem.at[7])
    part = gbuf[0]
    for i in range(1, CX):
        part = part + gbuf[i]
    cbuf[chipy] = part
    for dy in range(1, CY):
        y = lax.rem(chipy + dy, CY)
        remote(cbuf.at[chipy], cbuf.at[chipy], 9, at_chip(y, chipx), zme).start()

    lax.fori_loop(N // 2, N, back, 0)

    drain(cbuf, CY - 1, rsem.at[9])
    part = cbuf[0]
    for i in range(1, CY):
        part = part + cbuf[i]
    dgain_ref[...] = part

    def finish(h, incoming):
        lam = pows[0, h]
        pb = pows[1, h]
        state = lam * incoming
        for n in reversed(range(N)):
            rin = state.astype(BF16)
            w = jnp.where(segc[rows(n), :] == rlab[n], wl[h], 0.0)
            dk = dkp[rows(n), col(h)] + w * nt(vv[rows(n), col(h)], rin)
            dv = dvp[rows(n), col(h)] + w * nn(kv[rows(n), col(h)], rin)
            dkv[rows(n), col(h)] = dk.astype(BF16)
            dvv[rows(n), col(h)] = dv.astype(BF16)
            if n > 0:
                keep = rlab[n] == rlab[n - 1]
                state = jnp.where(keep, pb, 0.0) * state + lam * rst[n, h]

    lab_in1 = rbuf1[chipx + 1, SR : SR + 1, :]
    drain(ebuf1, CX - 1, rsem.at[8])
    kept = hand_over(1, fen1, ebuf1, lab_entry1, lab_in1, qbs1)
    rlab[N - 1] = lax.select(core == 1, lab_in1, lab_entry1)
    post1 = remote(qbs1, qbr1, 10, mate, zme)
    post1.start()
    for i in range(HH):
        finish(own0 + i, kept[i])
    post1.wait_recv()
    for i in range(HH):
        finish(other0 + i, qbr1[i * HD : (i + 1) * HD, :])
    for copy in (pair0, post0, pair1, post1, gain_pair):
        copy.wait_send()
    drain(rbuf0, 2 * CX - 1, ssem.at[1])
    drain(sbuf0, CX - 1, ssem.at[2])
    drain(zbuf, Z - 1, ssem.at[4])
    drain(rbuf1, 2 * CX - 1, ssem.at[6])
    drain(gbuf, CX - 1, ssem.at[7])
    drain(sbuf1, CX - 1, ssem.at[8])
    drain(cbuf, CY - 1, ssem.at[9])


def mover(pieces, *refs):
    half = len(refs) // 2
    sems = refs[-1]
    copies = []
    for i in range(half):
        src, dst = refs[i], refs[half + i]
        step = src.shape[0] // pieces[i]
        for j in range(pieces[i]):
            part = pl.ds(j * step, step)
            copies.append(pltpu.make_async_copy(src.at[part], dst.at[part], sems.at[len(copies)]))
    for copy in copies:
        copy.start()
    for copy in copies:
        copy.wait()


def body(queries, keys, values, gate, grad_out, gain, decay_rate, segment_ids):
    R = lax.axis_size("ctx")
    Z = lax.axis_size("head")
    T, W = queries.shape
    H = W // HD
    N = T // BLOCK
    CX = 4
    HR = H * HD // 2
    SR = HR // CX
    hbm = pl.BlockSpec(memory_space=pltpu.HBM)
    vspec = pl.BlockSpec(memory_space=pltpu.VMEM)
    big = jax.ShapeDtypeStruct((T, W), BF16)
    small = jax.ShapeDtypeStruct((1, W), F32)
    VM = pltpu.VMEM
    scratch = (
        [VM((T, W), BF16)] * 5
        + [
            VM((T, HD), F32),
            VM((H, BLOCK, HD), F32),
            VM((H, BLOCK, HD), F32),
            VM((H, BLOCK, BLOCK), F32),
            VM((N, H, HD, HD), F32),
            VM((N, H, BLOCK, BLOCK), BF16),
            VM((T, W), F32),
            VM((T, W), F32),
            VM((N, H, HD, HD), BF16),
            VM((BLOCK, 2 * N * HD), F32),
            VM((N, H, HD, BLOCK), BF16),
            VM((T, W), BF16),
            VM((N, H, HD, HD), F32),
            VM((T, W), F32),
            VM((T, W), F32),
            VM((T, HD), F32),
            VM((T, HD), F32),
            VM((T, W), BF16),
            VM((4, H, 1, HD), F32),
        ]
        + [VM((HR + 8, HD), F32)] * 2
        + [VM((HR, HD), F32)] * 2
        + [VM((CX, SR + 8, HD), F32), VM((2 * CX, SR + 8, HD), F32)]
        + [VM((CX, SR, HD), F32)] * 2
        + [VM((HR, HD), F32)] * 2
        + [VM((HR + 8, HD), F32)] * 2
        + [VM((HR, HD), F32)]
        + [VM((CX, SR + 8, HD), F32), VM((2 * CX, SR + 8, HD), F32)]
        + [VM((CX, SR, HD), F32)] * 2
        + [VM((HR, HD), F32)] * 2
        + [
            VM((N, 1, HD), F32),
            VM((N, 1, HD), F32),
            VM((Z, 2 * N, BLOCK), F32),
            VM((1, W), F32),
            VM((1, W), F32),
            VM((CX, 1, W), F32),
            VM((R // (2 * CX), 1, W), F32),
            pltpu.SemaphoreType.DMA((7,)),
            pltpu.SemaphoreType.DMA((12,)),
            pltpu.SemaphoreType.DMA((12,)),
        ]
    )
    rates = jnp.broadcast_to(decay_rate[:, None], (H, HD))
    small_in = jnp.concatenate([gain.reshape(H, HD), rates], axis=0)
    outs = pl.pallas_call(
        functools.partial(kernel, (R, Z, N, H)),
        out_shape=(big, big, big, big, small),
        in_specs=[hbm] * 5 + [vspec] * 2,
        out_specs=(vspec,) * 5,
        scratch_shapes=scratch,
        compiler_params=pltpu.CompilerParams(
            collective_id=0, has_side_effects=True, vmem_limit_bytes=VMEM_A
        ),
    )(
        queries, keys, values, gate, grad_out,
        small_in, segment_ids.reshape(1, T),
    )
    pieces = (4, 4, 4, 4, 1)
    moved = pl.pallas_call(
        functools.partial(mover, pieces),
        out_shape=(big, big, big, big, small),
        in_specs=[vspec] * 5,
        out_specs=(hbm,) * 5,
        scratch_shapes=[pltpu.SemaphoreType.DMA((sum(pieces),))],
        compiler_params=pltpu.CompilerParams(vmem_limit_bytes=VMEM_B),
    )(*outs)
    dq, dk, dv, gg, dgain = moved
    return dq, dk, dv, gg, dgain.reshape(W)


def solution(mesh):
    in_specs = (P("ctx", "head"),) * 5 + (P("head"), P("head"), P("ctx"))
    out_specs = (P("ctx", "head"),) * 4 + (P("head"),)
    return jax.shard_map(body, mesh=mesh, in_specs=in_specs, out_specs=out_specs, check_vma=False)
```

```python
import functools

import jax
import jax.numpy as jnp
from jax import lax
from jax.experimental import pallas as pl
from jax.experimental.pallas import tpu as pltpu
from jax.sharding import PartitionSpec as P

MESH = pl.DeviceIdType.MESH
F32 = jnp.float32
BF16 = jnp.bfloat16
BLOCK = 256
HD = 128
EPS = 1e-06
VMEM_A = 49 * 1024 * 1024
VMEM_B = 8 * 1024 * 1024


def nn(a, b):
    return lax.dot_general(a, b, (((1,), (0,)), ((), ())), preferred_element_type=F32)


def nt(a, b):
    return lax.dot_general(a, b, (((1,), (1,)), ((), ())), preferred_element_type=F32)


def tn(a, b):
    return lax.dot_general(a, b, (((0,), (0,)), ((), ())), preferred_element_type=F32)


def drain(ref, count, sem):
    if count == 0:
        return
    part = ref.at[pl.ds(0, count)]
    pltpu.make_async_copy(part, part, sem).wait()


def kernel(
    dims,
    q_hbm, k_hbm, v_hbm, g_hbm, o_hbm, small_ref, seg_ref,
    dqv, dkv, dvv, ggv, dgain_ref,
    qv, kv, vv, gv, ov,
    segc, wl, wf, wb, fst, sw, attn, dzs, sst, bc, qwt, datt, rst, dkp, dvp, ssq, sda, qc, pows,
    pbs0, pbr0, hfs, fen, fbuf0, rbuf0, sbuf0, ebuf0, qbs0, qbr0,
    pbs1, pbr1, fen1, fbuf1, rbuf1, sbuf1, ebuf1, qbs1, qbr1,
    flab, rlab, zbuf, gps, gpr, gbuf, cbuf,
    in_sem, ssem, rsem,
):
    R, Z, N, H = dims
    T = N * BLOCK
    C = R // 2
    HH = H // 2
    HR = HH * HD
    CX = 4
    SR = HR // CX
    HJ = CX // HH
    CY = C // CX
    me = lax.axis_index("ctx")
    zme = lax.axis_index("head")
    core = lax.rem(me, 2)
    mate = me + 1 - 2 * core
    chip = me // 2
    chipy = chip // CX
    chipx = lax.rem(chip, CX)
    own0 = HH * core
    other0 = HH * (1 - core)

    def half(ref, h0):
        return ref.at[:, pl.ds(pl.multiple_of(h0 * HD, HR), HR)]

    loads = [
        pltpu.make_async_copy(src, dst, in_sem.at[i])
        for i, (src, dst) in enumerate(
            (
                (half(k_hbm, other0), half(kv, other0)), (half(v_hbm, other0), half(vv, other0)),
                (half(k_hbm, own0), half(kv, own0)), (half(v_hbm, own0), half(vv, own0)),
                (q_hbm, qv), (g_hbm, gv), (o_hbm, ov),
            )
        )
    ]
    for copy in loads[:4]:
        copy.start()

    barrier = pltpu.get_barrier_semaphore()

    def greet(ctx, head):
        pl.semaphore_signal(barrier, inc=1, device_id=(ctx, head), device_id_type=MESH)

    heads = sorted(range(1, Z), key=lambda i: min(i, Z - i), reverse=True)
    near = {(dy, dx) for dy in (0, 1, CY - 1) for dx in range(CX)}
    near = sorted((near | {(dy, 0) for dy in range(CY)}) - {(0, 0)}, reverse=True)
    for i in heads:
        greet(me, lax.rem(zme + i, Z))
    for dy, dx in near:
        y, x = lax.rem(chipy + dy, CY), lax.rem(chipx + dx, CX)
        greet(2 * (y * CX + x) + core, zme)
    greet(mate, zme)
    greeted = len(heads) + len(near) + 1
    for copy in loads[4:]:
        copy.start()

    def remote(src, dst, phase, ctx, head):
        return pltpu.make_async_remote_copy(
            src_ref=src, dst_ref=dst, send_sem=ssem.at[phase], recv_sem=rsem.at[phase],
            device_id=(ctx, head), device_id_type=MESH,
        )

    def col(h):
        start = h * HD
        return pl.ds(start if isinstance(h, int) else pl.multiple_of(start, HD), HD)

    def rows(n):
        start = n * BLOCK
        return pl.ds(start if isinstance(n, int) else pl.multiple_of(start, BLOCK), BLOCK)

    def rate(h):
        return small_ref[H + h : H + h + 1, :]

    def gain(h):
        return small_ref[h : h + 1, :]

    def power(h, times):
        return jnp.exp(rate(h) * -times)

    iota = lax.broadcasted_iota(jnp.int32, (BLOCK, HD), 0).astype(F32)
    first_row = jnp.where(lax.broadcasted_iota(jnp.int32, (16, HD), 0) == 0, 1.0, 0.0).astype(BF16)
    for n in range(N):
        seg = jnp.broadcast_to(seg_ref[0:1, rows(n)].astype(F32), (16, BLOCK)).astype(BF16)
        segc[rows(n), :] = tn(seg, first_row)
    for h in range(H):
        wl[h] = jnp.exp(-rate(h) * (BLOCK - 1.0 - iota))
        for i, times in enumerate((1.0, float(BLOCK), float(T), 2.0 * T)):
            pows[i, h] = power(h, times)
    mylast = segc[T - 1 : T, :]
    myfirst = segc[0:1, :]

    def at_chip(y, x):
        return 2 * (y * CX + x) + core

    around = (2, 1, 3)

    def merge(entry, pbr, lab_m, lab_p, fen_ref, fbuf):
        is_entry = core == entry
        lab_entry = lax.select(is_entry, lab_m, lab_p)
        lab_exit = lax.select(is_entry, lab_p, lab_m)
        for i in range(HH):
            part = slice(i * HD, (i + 1) * HD)
            fm = hfs[part, :]
            fp = pbr[part, :]
            fe = lax.select(is_entry, fm, fp)
            fx = lax.select(is_entry, fp, fm)
            fen_ref[part, :] = fe
            c = fx + jnp.where(lab_entry == lab_exit, pows[2, own0 + i], 0.0) * fe
            fbuf[i * HJ : (i + 1) * HJ, 0:SR, :] = c.reshape(HJ, SR, HD)
        return lab_entry, lab_exit

    def hand_over(entry, fen_ref, ebuf, lab_entry, lab_in, qbs):
        is_entry = core == entry
        kept = []
        for i in range(HH):
            part = slice(i * HD, (i + 1) * HD)
            ve = ebuf[i * HJ : (i + 1) * HJ].reshape(HD, HD)
            linked = jnp.where(lab_in == lab_entry, pows[2, own0 + i], 0.0)
            vx = fen_ref[part, :] + linked * ve
            qbs[part, :] = lax.select(is_entry, vx, ve)
            kept.append(lax.select(is_entry, ve, vx))
        return kept

    def device_state(h):
        own = None
        pb = pows[1, h]
        w = wl[h]
        for n in range(N):
            last = segc[n * BLOCK + BLOCK - 1 : n * BLOCK + BLOCK, :]
            here = segc[rows(n), :] == last
            kw = jnp.where(here, kv[rows(n), col(h)].astype(F32) * w, 0.0).astype(BF16)
            f = tn(kw, vv[rows(n), col(h)])
            fst[n, h] = f
            if own is None:
                own = f
            else:
                before = segc[n * BLOCK - 1 : n * BLOCK, :]
                own = jnp.where(before == last, pb, 0.0) * own + f
        return own

    loads[0].wait()
    loads[1].wait()
    for i in range(HH):
        pbs0[i * HD : (i + 1) * HD, :] = device_state(other0 + i)
    top = lax.broadcasted_iota(jnp.int32, (8, HD), 0) == 0
    pbs0[HR : HR + 8, :] = jnp.where(top, mylast, myfirst)
    pl.semaphore_wait(barrier, greeted)
    pair0 = remote(pbs0, pbr0, 0, mate, zme)
    pair0.start()
    loads[2].wait()
    loads[3].wait()
    for i in range(HH):
        hfs[i * HD : (i + 1) * HD, :] = device_state(own0 + i)
    pair0.wait_recv()
    matelast = pbr0[HR : HR + 1, :]
    matefirst = pbr0[HR + 1 : HR + 2, :]
    lab_entry0, lab_exit0 = merge(0, pbr0, mylast, matelast, fen, fbuf0)
    for x in range(CX):
        fbuf0[x, SR : SR + 1, :] = lab_exit0

    def scatter(fbuf, rbuf, phase, turn_y, near, far):
        there = lax.rem(chipy + turn_y, CY)
        for dx in (2, 1, 3, 0):
            x = lax.rem(chipx + dx, CX)
            remote(fbuf.at[x], rbuf.at[far + chipx], phase, at_chip(there, x), zme).start()
        for dx in around:
            x = lax.rem(chipx + dx, CX)
            remote(fbuf.at[x], rbuf.at[near + chipx], phase, at_chip(chipy, x), zme).start()
        rbuf[near + chipx] = fbuf[chipx]

    def spread(sbuf, ebuf, phase):
        for dx in around:
            x = lax.rem(chipx + dx, CX)
            remote(sbuf.at[x], ebuf.at[chipx], phase, at_chip(chipy, x), zme).start()
        ebuf[chipx] = sbuf[chipx]

    scatter(fbuf0, rbuf0, 1, 1, CX, 0)

    d2 = (
        lax.broadcasted_iota(jnp.int32, (BLOCK, BLOCK), 0)
        - lax.broadcasted_iota(jnp.int32, (BLOCK, BLOCK), 1)
    ).astype(F32)
    for h in range(H):
        wf[h] = jnp.exp(-rate(h) * iota)
        rate2 = jnp.concatenate([rate(h), rate(h)], axis=1)
        wb[h] = jnp.where(d2 >= 0, jnp.exp(-rate2 * jnp.maximum(d2, 0.0)), 0.0)

    def same_of(n):
        sc = segc[rows(n), :]
        return jnp.concatenate([sc, sc], axis=1) == seg_ref[0:1, rows(n)].astype(F32)

    def intra(n, c):
        same = same_of(n)
        for h in range(H):
            s = nt(qv[rows(n), col(h)], kv[rows(n), col(h)])
            s = jnp.where(same, s * wb[h], 0.0).astype(BF16)
            sw[n, h] = s
            attn[rows(n), col(h)] = nn(s, vv[rows(n), col(h)])
            sig = jax.nn.sigmoid(gv[rows(n), col(h)].astype(F32))
            dzs[rows(n), col(h)] = ov[rows(n), col(h)].astype(F32) * sig * gain(h)
        return c

    for copy in loads[4:]:
        copy.wait()
    lax.fori_loop(0, N // 2, intra, 0)

    pchip = pows[3, own0 + chipx // HJ]
    drain(rbuf0, 2 * CX - 1, rsem.at[1])
    acc = rbuf0[0, 0:SR, :]
    for i in range(1, 2 * CX):
        if i >= CX:
            sbuf0[i - CX] = acc
        if i < 2 * CX - 1:
            linked = rbuf0[i - 1, SR : SR + 1, :] == rbuf0[i, SR : SR + 1, :]
            acc = rbuf0[i, 0:SR, :] + jnp.where(linked, pchip, 0.0) * acc
    spread(sbuf0, ebuf0, 2)

    lab_in0 = rbuf0[CX - 1 + chipx, SR : SR + 1, :]
    flab[0] = lax.select(core == 0, lab_in0, lab_entry0)
    for n in range(1, N):
        flab[n] = segc[n * BLOCK - 1 : n * BLOCK, :]
        rlab[n - 1] = segc[n * BLOCK : n * BLOCK + 1, :]

    def decayed(n, c):
        linked = segc[rows(n), :] == flab[n]
        for h in range(H):
            qd = jnp.where(linked, qv[rows(n), col(h)].astype(F32) * wf[h], 0.0)
            qc[rows(n), col(h)] = qd.astype(BF16)
        return c

    lax.fori_loop(N // 2, N, intra, 0)
    lax.fori_loop(0, N, decayed, 0)

    def chain(h, incoming):
        lam = pows[0, h]
        pb = pows[1, h]
        state = lam * incoming
        for n in range(N):
            sst[n, h] = state.astype(BF16)
            if n < N - 1:
                keep = flab[n] == flab[n + 1]
                state = jnp.where(keep, pb, 0.0) * state + lam * fst[n, h]

    row16 = lax.broadcasted_iota(jnp.int32, (16, HD), 0)

    def cross(n, h0):
        sq = jnp.zeros((BLOCK, HD), F32)
        da = jnp.zeros((BLOCK, HD), F32)
        for i in range(HH):
            h = h0 + i
            a = attn[rows(n), col(h)] + nn(qc[rows(n), col(h)], sst[n, h])
            attn[rows(n), col(h)] = a
            sq = sq + a * a
            da = da + dzs[rows(n), col(h)] * a
        return sq, da

    def cross_own(n, c):
        sq, da = cross(n, own0)
        ssq[rows(n), :] = sq
        sda[rows(n), :] = da
        return c

    def cross_other(n, total):
        sq, da = cross(n, other0)
        pick1 = jnp.where(row16 == n, 1.0, 0.0).astype(BF16)
        pick2 = jnp.where(row16 == n + N, 1.0, 0.0).astype(BF16)
        sq = (sq + ssq[rows(n), :]).astype(BF16)
        da = (da + sda[rows(n), :]).astype(BF16)
        return total + nt(pick1, sq) + nt(pick2, da)

    drain(ebuf0, CX - 1, rsem.at[2])
    kept = hand_over(0, fen, ebuf0, lab_entry0, lab_in0, qbs0)
    post0 = remote(qbs0, qbr0, 3, mate, zme)
    post0.start()
    for i in range(HH):
        chain(own0 + i, kept[i])
    for n in range(N):
        cross_own(n, 0)
    post0.wait_recv()
    for i in range(HH):
        chain(other0 + i, qbr0[i * HD : (i + 1) * HD, :])
    total = jnp.zeros((16, BLOCK), F32)
    for n in range(N):
        total = cross_other(n, total)
    zbuf[zme] = total[0 : 2 * N, :]

    for i in heads:
        remote(zbuf.at[zme], zbuf.at[zme], 4, me, lax.rem(zme + i, Z)).start()

    def turn(n, c):
        first = segc[pl.ds(n * BLOCK, 1), :]
        here = segc[rows(n), :] == first
        for h in range(H):
            qw = jnp.where(here, qv[rows(n), col(h)].astype(F32) * wf[h], 0.0)
            qwt[n, h] = qw.T.astype(BF16)
        return c

    lax.fori_loop(0, N, turn, 0)

    feats = float(H * HD * Z)
    wide = 2 * N * HD
    rr = lax.broadcasted_iota(jnp.int32, (4 * N, wide), 0)
    cc = lax.broadcasted_iota(jnp.int32, (4 * N, wide), 1) // HD
    picks = jnp.where((rr == cc) | (rr == cc + 2 * N), 1.0, 0.0).astype(BF16)
    drain(zbuf, Z - 1, rsem.at[4])
    tot = zbuf[0]
    for i in range(1, Z):
        tot = tot + zbuf[i]
    rat = lax.rsqrt(tot[0:N] / feats + EPS)
    cor = rat * rat * rat * (tot[N : 2 * N] / feats)
    both = jnp.concatenate([rat, cor], axis=0)
    upper = both.astype(BF16).astype(F32)
    lhs = jnp.concatenate([upper, both - upper], axis=0).astype(BF16)
    bc[...] = tn(lhs, picks)

    def factor(n):
        if isinstance(n, int):
            return bc[:, n * HD : (n + 1) * HD]
        return bc[:, pl.ds(pl.multiple_of(n * HD, HD), HD)]

    def reverse_state(h):
        own = None
        pb = pows[1, h]
        for n in reversed(range(N)):
            d = (factor(n) * dzs[rows(n), col(h)] - factor(N + n) * attn[rows(n), col(h)]).astype(BF16)
            datt[rows(n), col(h)] = d
            f = nn(qwt[n, h], d)
            rst[n, h] = f
            if own is None:
                own = f
            else:
                first = segc[n * BLOCK : n * BLOCK + 1, :]
                after = segc[(n + 1) * BLOCK : (n + 1) * BLOCK + 1, :]
                own = jnp.where(first == after, pb, 0.0) * own + f
        return own

    for i in range(HH):
        pbs1[i * HD : (i + 1) * HD, :] = reverse_state(other0 + i)
    pair1 = remote(pbs1, pbr1, 5, mate, zme)
    pair1.start()
    for i in range(HH):
        hfs[i * HD : (i + 1) * HD, :] = reverse_state(own0 + i)
    pair1.wait_recv()
    lab_entry1, lab_exit1 = merge(1, pbr1, myfirst, matefirst, fen1, fbuf1)
    for x in range(CX):
        fbuf1[x, SR : SR + 1, :] = lab_exit1
    scatter(fbuf1, rbuf1, 6, CY - 1, 0, CX)

    def gated(n, sums):
        out = []
        for h in range(H):
            normed = attn[rows(n), col(h)] * factor(n)
            sig = jax.nn.sigmoid(gv[rows(n), col(h)].astype(F32))
            t = ov[rows(n), col(h)].astype(F32) * sig * normed
            ggv[rows(n), col(h)] = (t * gain(h) * (1.0 - sig)).astype(BF16)
            out.append(sums[h] + jnp.sum(t.reshape(BLOCK // 8, 8, HD), axis=0))
        return tuple(out)

    sums = lax.fori_loop(0, N, gated, tuple(jnp.zeros((8, HD), F32) for _ in range(H)))
    gps[...] = jnp.concatenate([jnp.sum(s, axis=0, keepdims=True) for s in sums], axis=1)
    gain_pair = remote(gps, gpr, 11, mate, zme)
    gain_pair.start()

    def back(n, c):
        same = same_of(n)
        linked = segc[rows(n), :] == flab[n]
        for h in range(H):
            d = datt[rows(n), col(h)]
            s = nt(d, vv[rows(n), col(h)])
            ds = jnp.where(same, s * wb[h], 0.0).astype(BF16)
            dq = nn(ds, kv[rows(n), col(h)])
            dq = dq + jnp.where(linked, wf[h], 0.0) * nt(d, sst[n, h])
            dqv[rows(n), col(h)] = dq.astype(BF16)
            dkp[rows(n), col(h)] = tn(ds, qv[rows(n), col(h)])
            dvp[rows(n), col(h)] = tn(sw[n, h], d)
        return c

    lax.fori_loop(0, 1, back, 0)
    gain_pair.wait_recv()
    gbuf[chipx] = gps[...] + gpr[...]
    for dx in around:
        x = lax.rem(chipx + dx, CX)
        remote(gbuf.at[chipx], gbuf.at[chipx], 7, at_chip(chipy, x), zme).start()
    lax.fori_loop(1, N // 2, back, 0)

    drain(rbuf1, 2 * CX - 1, rsem.at[6])
    acc = rbuf1[2 * CX - 1, 0:SR, :]
    for i in reversed(range(2 * CX - 1)):
        if i < CX:
            sbuf1[i] = acc
        if i > 0:
            linked = rbuf1[i + 1, SR : SR + 1, :] == rbuf1[i, SR : SR + 1, :]
            acc = rbuf1[i, 0:SR, :] + jnp.where(linked, pchip, 0.0) * acc
    spread(sbuf1, ebuf1, 8)

    drain(gbuf, CX - 1, rsem.at[7])
    part = gbuf[0]
    for i in range(1, CX):
        part = part + gbuf[i]
    cbuf[chipy] = part
    for dy in range(1, CY):
        y = lax.rem(chipy + dy, CY)
        remote(cbuf.at[chipy], cbuf.at[chipy], 9, at_chip(y, chipx), zme).start()

    lax.fori_loop(N // 2, N, back, 0)

    drain(cbuf, CY - 1, rsem.at[9])
    part = cbuf[0]
    for i in range(1, CY):
        part = part + cbuf[i]
    dgain_ref[...] = part

    def finish(h, incoming):
        lam = pows[0, h]
        pb = pows[1, h]
        state = lam * incoming
        for n in reversed(range(N)):
            rin = state.astype(BF16)
            w = jnp.where(segc[rows(n), :] == rlab[n], wl[h], 0.0)
            dk = dkp[rows(n), col(h)] + w * nt(vv[rows(n), col(h)], rin)
            dv = dvp[rows(n), col(h)] + w * nn(kv[rows(n), col(h)], rin)
            dkv[rows(n), col(h)] = dk.astype(BF16)
            dvv[rows(n), col(h)] = dv.astype(BF16)
            if n > 0:
                keep = rlab[n] == rlab[n - 1]
                state = jnp.where(keep, pb, 0.0) * state + lam * rst[n, h]

    lab_in1 = rbuf1[chipx + 1, SR : SR + 1, :]
    drain(ebuf1, CX - 1, rsem.at[8])
    kept = hand_over(1, fen1, ebuf1, lab_entry1, lab_in1, qbs1)
    rlab[N - 1] = lax.select(core == 1, lab_in1, lab_entry1)
    post1 = remote(qbs1, qbr1, 10, mate, zme)
    post1.start()
    for i in range(HH):
        finish(own0 + i, kept[i])
    post1.wait_recv()
    for i in range(HH):
        finish(other0 + i, qbr1[i * HD : (i + 1) * HD, :])
    for copy in (pair0, post0, pair1, post1, gain_pair):
        copy.wait_send()
    drain(rbuf0, 2 * CX - 1, ssem.at[1])
    drain(sbuf0, CX - 1, ssem.at[2])
    drain(zbuf, Z - 1, ssem.at[4])
    drain(rbuf1, 2 * CX - 1, ssem.at[6])
    drain(gbuf, CX - 1, ssem.at[7])
    drain(sbuf1, CX - 1, ssem.at[8])
    drain(cbuf, CY - 1, ssem.at[9])


def mover(pieces, *refs):
    half = len(refs) // 2
    sems = refs[-1]
    copies = []
    for i in range(half):
        src, dst = refs[i], refs[half + i]
        step = src.shape[0] // pieces[i]
        for j in range(pieces[i]):
            part = pl.ds(j * step, step)
            copies.append(pltpu.make_async_copy(src.at[part], dst.at[part], sems.at[len(copies)]))
    for copy in copies:
        copy.start()
    for copy in copies:
        copy.wait()


def body(queries, keys, values, gate, grad_out, gain, decay_rate, segment_ids):
    R = lax.axis_size("ctx")
    Z = lax.axis_size("head")
    T, W = queries.shape
    H = W // HD
    N = T // BLOCK
    CX = 4
    HR = H * HD // 2
    SR = HR // CX
    hbm = pl.BlockSpec(memory_space=pltpu.HBM)
    vspec = pl.BlockSpec(memory_space=pltpu.VMEM)
    big = jax.ShapeDtypeStruct((T, W), BF16)
    small = jax.ShapeDtypeStruct((1, W), F32)
    VM = pltpu.VMEM
    scratch = (
        [VM((T, W), BF16)] * 5
        + [
            VM((T, HD), F32),
            VM((H, BLOCK, HD), F32),
            VM((H, BLOCK, HD), F32),
            VM((H, BLOCK, BLOCK), F32),
            VM((N, H, HD, HD), F32),
            VM((N, H, BLOCK, BLOCK), BF16),
            VM((T, W), F32),
            VM((T, W), F32),
            VM((N, H, HD, HD), BF16),
            VM((BLOCK, 2 * N * HD), F32),
            VM((N, H, HD, BLOCK), BF16),
            VM((T, W), BF16),
            VM((N, H, HD, HD), F32),
            VM((T, W), F32),
            VM((T, W), F32),
            VM((T, HD), F32),
            VM((T, HD), F32),
            VM((T, W), BF16),
            VM((4, H, 1, HD), F32),
        ]
        + [VM((HR + 8, HD), F32)] * 2
        + [VM((HR, HD), F32)] * 2
        + [VM((CX, SR + 8, HD), F32), VM((2 * CX, SR + 8, HD), F32)]
        + [VM((CX, SR, HD), F32)] * 2
        + [VM((HR, HD), F32)] * 2
        + [VM((HR + 8, HD), F32)] * 2
        + [VM((HR, HD), F32)]
        + [VM((CX, SR + 8, HD), F32), VM((2 * CX, SR + 8, HD), F32)]
        + [VM((CX, SR, HD), F32)] * 2
        + [VM((HR, HD), F32)] * 2
        + [
            VM((N, 1, HD), F32),
            VM((N, 1, HD), F32),
            VM((Z, 2 * N, BLOCK), F32),
            VM((1, W), F32),
            VM((1, W), F32),
            VM((CX, 1, W), F32),
            VM((R // (2 * CX), 1, W), F32),
            pltpu.SemaphoreType.DMA((7,)),
            pltpu.SemaphoreType.DMA((12,)),
            pltpu.SemaphoreType.DMA((12,)),
        ]
    )
    rates = jnp.broadcast_to(decay_rate[:, None], (H, HD))
    small_in = jnp.concatenate([gain.reshape(H, HD), rates], axis=0)
    outs = pl.pallas_call(
        functools.partial(kernel, (R, Z, N, H)),
        out_shape=(big, big, big, big, small),
        in_specs=[hbm] * 5 + [vspec] * 2,
        out_specs=(vspec,) * 5,
        scratch_shapes=scratch,
        compiler_params=pltpu.CompilerParams(
            collective_id=0, has_side_effects=True, vmem_limit_bytes=VMEM_A
        ),
    )(
        queries, keys, values, gate, grad_out,
        small_in, segment_ids.reshape(1, T),
    )
    pieces = (1, 1, 1, 1, 1)
    moved = pl.pallas_call(
        functools.partial(mover, pieces),
        out_shape=(big, big, big, big, small),
        in_specs=[vspec] * 5,
        out_specs=(hbm,) * 5,
        scratch_shapes=[pltpu.SemaphoreType.DMA((sum(pieces),))],
        compiler_params=pltpu.CompilerParams(vmem_limit_bytes=VMEM_B),
    )(*outs)
    dq, dk, dv, gg, dgain = moved
    return dq, dk, dv, gg, dgain.reshape(W)


def solution(mesh):
    in_specs = (P("ctx", "head"),) * 5 + (P("head"), P("head"), P("ctx"))
    out_specs = (P("ctx", "head"),) * 4 + (P("head"),)
    return jax.shard_map(body, mesh=mesh, in_specs=in_specs, out_specs=out_specs, check_vma=False)
```
